128 devices in a mesh: segment: 2 (over x_lo), tr: 8 (over x_hi, y), tc: 8 (over z, core).
Axes of the slice: x: 4 (x_hi: 2, x_lo: 2; x = x_hi * 2 + x_lo), y: 4, z: 4, core: 2. Of those that a mesh axis runs over, the one named last changes fastest.
Arguments:
- features: bfloat16 [2, 8192, 1280], P('segment', ('tr', 'tc')), may hold values from -6 to 6
- attn_hidden: bfloat16 [2, 8192, 1280], P('segment', ('tr', 'tc')), may hold values from -0.125 to 0.125
- first_deconv: bfloat16 [1280, 2, 2, 640], P('segment'), may hold values from -0.15625 to 0.15625
- first_bias: float32 [640], replicated, may hold values from -3 to 3
- mid_gain: float32 [640], replicated, may hold values from 0.1 to 1.9
- mid_shift: float32 [640], replicated, may hold values from -1.75 to 1.75
- second_deconv: bfloat16 [640, 2, 2, 320], replicated, may hold values from -0.25 to 0.25
- second_bias: float32 [320], replicated, may hold values from -3 to 3
- half_deconv: bfloat16 [1280, 2, 2, 640], P('segment'), may hold values from -0.15625 to 0.15625
- half_bias: float32 [640], replicated, may hold values from -3 to 3
- lateral_four: bfloat16 [320, 256], replicated, may hold values from -0.3125 to 0.3125
- lateral_eight: bfloat16 [640, 256], replicated, may hold values from -0.25 to 0.25
- lateral_sixteen: bfloat16 [1280, 256], replicated, may hold values from -0.15625 to 0.15625
- lateral_coarse: bfloat16 [1280, 256], replicated, may hold values from -0.15625 to 0.15625
- output_conv: bfloat16 [4, 3, 3, 256, 256], replicated, may hold values from -0.125 to 0.125
- level_gain: float32 [4, 2, 256], replicated, may hold values from 0.1 to 1.9
- level_shift: float32 [4, 2, 256], replicated, may hold values from -1.75 to 1.75
- cotangent_four: bfloat16 [2, 512, 256, 256], P('segment', 'tr', 'tc'), may hold values from -6 to 6
- cotangent_eight: bfloat16 [2, 256, 128, 256], P('segment', 'tr', 'tc'), may hold values from -6 to 6
- cotangent_sixteen: bfloat16 [2, 128, 64, 256], P('segment', 'tr', 'tc'), may hold values from -6 to 6
- cotangent_coarse: bfloat16 [2, 64, 32, 256], P('segment', 'tr', 'tc'), may hold values from -6 to 6
Outputs:
- level_four: bfloat16 [2, 512, 256, 256], P('segment', 'tr', 'tc')
- level_eight: bfloat16 [2, 256, 128, 256], P('segment', 'tr', 'tc')
- level_sixteen: bfloat16 [2, 128, 64, 256], P('segment', 'tr', 'tc')
- level_coarse: bfloat16 [2, 64, 32, 256], P('segment', 'tr', 'tc')
- feature_grad: bfloat16 [2, 8192, 1280], P('segment', ('tr', 'tc'))
- weight_grad: float32 [1280, 1280], P(('segment', 'tr', 'tc'))
The draws below stay inside these ranges and needn't reach their ends.
All inputs are finite; a program needn't handle non-finite values.
Results may differ from the reference program's by a relative error of at most 0.02.
Values may be sent and summed in bfloat16 or wider, within the bound.
A program may use at most 128 MiB of HBM per device.

```python
import jax
import jax.numpy as jnp
from jax import lax

D = 1280
CN = 256
C_MID = 640
C_FINE = 320
H = 128
W = 64
TOKENS = 8192
N_SEGMENT = 2


def with_spikes(array, own_key, source, target, shards_of, factor):
    owner, partner = [(jnp.arange(array.shape[position]) // (array.shape[position] // shards_of)).reshape([-1 if axis == position else 1 for axis in range(array.ndim)]) for position in (source, target)]
    chosen = jax.random.permutation(own_key, shards_of)[partner]
    strong = (owner == chosen) | (owner == (partner + shards_of // 2) % shards_of)
    return jnp.where(strong, factor * array, array)


def block_scale(rng, dims, pieces, smallest, high):
    def one(axis_at, parts):
        heights = jax.random.uniform(jax.random.fold_in(jax.random.fold_in(rng, 6), axis_at), (parts,), jnp.float32, smallest / len(pieces), high / len(pieces))
        return jnp.repeat(jnp.exp(heights), dims[axis_at] // parts).reshape((-1,) + (1,) * (len(dims) - axis_at - 1))

    level = one(*pieces[0])
    for cut in pieces[1:]:
        level = level * one(*cut)
    return level


def bell_draw(key, extent, scale, limit, shards=(), held_as=jnp.bfloat16):
    array = scale * jax.random.normal(key, extent, jnp.float32)
    if shards:
        array = array * block_scale(key, extent, shards, -0.22, 0.18)
    return jnp.clip(array, -limit, limit).astype(held_as)


def bell_draw_with(own_key, extent, scale, reach, split, heavy, dtype=jnp.bfloat16):
    entries = scale * jax.random.normal(own_key, extent, jnp.float32)
    if split:
        entries = entries * block_scale(own_key, extent, split, -0.22, 0.18)
    return jnp.clip(with_spikes(entries, jax.random.fold_in(own_key, 3), *heavy), -reach, reach).astype(dtype)


def setup_inputs(seed: int = 0) -> dict:
    arg_keys = jax.random.split(jax.random.key(seed), 22)
    return {
        "features": bell_draw(arg_keys[0], (N_SEGMENT, TOKENS, D), 1.0, 6.0, ((0, 2), (1, 64))),
        "attn_hidden": bell_draw_with(arg_keys[1], (N_SEGMENT, TOKENS, D), ((2 * TOKENS) ** -0.5), 0.125, ((0, 2), (1, 64)), (1, 2, 64, 4.0)),
        "first_deconv": bell_draw(arg_keys[2], (D, 2, 2, C_MID), D ** -0.5, 0.15625, ((0, 2),)),
        "first_bias": bell_draw(arg_keys[3], (C_MID,), 0.5, 3.0, (), jnp.float32),
        "mid_gain": jnp.clip(1.0 + 0.18 * jax.random.normal(arg_keys[4], (C_MID,), jnp.float32), 0.1, 1.9),
        "mid_shift": bell_draw(arg_keys[5], (C_MID,), 0.3, 1.75, (), jnp.float32),
        "second_deconv": bell_draw(arg_keys[6], (C_MID, 2, 2, C_FINE), C_MID ** -0.5, 0.25),
        "second_bias": bell_draw(arg_keys[7], (C_FINE,), 0.5, 3.0, (), jnp.float32),
        "half_deconv": bell_draw(arg_keys[8], (D, 2, 2, C_MID), D ** -0.5, 0.15625, ((0, 2),)),
        "half_bias": bell_draw(arg_keys[9], (C_MID,), 0.5, 3.0, (), jnp.float32),
        "lateral_four": bell_draw(arg_keys[10], (C_FINE, CN), C_FINE ** -0.5, 0.3125),
        "lateral_eight": bell_draw(arg_keys[11], (C_MID, CN), C_MID ** -0.5, 0.25),
        "lateral_sixteen": bell_draw(arg_keys[12], (D, CN), D ** -0.5, 0.15625),
        "lateral_coarse": bell_draw(arg_keys[13], (D, CN), D ** -0.5, 0.15625),
        "output_conv": bell_draw(arg_keys[14], (4, 3, 3, CN, CN), (9 * CN) ** -0.5, 0.125),
        "level_gain": jnp.clip(1.0 + 0.18 * jax.random.normal(arg_keys[15], (4, 2, CN), jnp.float32), 0.1, 1.9),
        "level_shift": bell_draw(arg_keys[16], (4, 2, CN), 0.3, 1.75, (), jnp.float32),
        "cotangent_four": bell_draw(arg_keys[17], (N_SEGMENT, 4 * H, 4 * W, CN), 1.0, 6.0, ((0, 2), (1, 8), (2, 8))),
        "cotangent_eight": bell_draw(arg_keys[18], (N_SEGMENT, 2 * H, 2 * W, CN), 1.0, 6.0, ((0, 2), (1, 8), (2, 8))),
        "cotangent_sixteen": bell_draw(arg_keys[19], (N_SEGMENT, H, W, CN), 1.0, 6.0, ((0, 2), (1, 8), (2, 8))),
        "cotangent_coarse": bell_draw(arg_keys[20], (N_SEGMENT, H // 2, W // 2, CN), 1.0, 6.0, ((0, 2), (1, 8), (2, 8))),
    }


EPS = 1e-06

def expand_pixels(pixels, weight, offset):
    height, breadth, channels = pixels.shape
    outward = weight.shape[3]
    flattened = jnp.dot(pixels.reshape(height * breadth, channels), weight.reshape(channels, 4 * outward), preferred_element_type=jnp.float32)
    blocks = flattened.reshape(height, breadth, 2, 2, outward) + offset
    return blocks.transpose(0, 2, 1, 3, 4).reshape(2 * height, 2 * breadth, outward)

def layer_norm(values, factor, offset):
    centre = lax.optimization_barrier(jnp.mean(values, axis=-1, keepdims=True))
    spread = lax.optimization_barrier(jnp.mean(jnp.square(values - centre), axis=-1, keepdims=True))
    return (values - centre) * lax.rsqrt(spread + EPS) * factor + offset

def lateral(pixels, weight, factor, offset):
    height, breadth, channels = pixels.shape
    projected = jnp.dot(pixels.reshape(height * breadth, channels), weight, preferred_element_type=jnp.float32)
    return layer_norm(projected, factor, offset).reshape(height, breadth, weight.shape[1])

def lift_levels(feature32, weights):
    first_deconv, first_bias, mid_gain, mid_shift, second_deconv, second_bias, half_deconv, half_bias, laterals, level_gain, level_shift = weights
    tokens = feature32.astype(jnp.bfloat16)
    height, breadth, channels = tokens.shape
    upsampled = expand_pixels(tokens, first_deconv, first_bias)
    upsampled = jax.nn.gelu(layer_norm(upsampled, mid_gain, mid_shift), approximate=False).astype(jnp.bfloat16)
    finest = expand_pixels(upsampled, second_deconv, second_bias).astype(jnp.bfloat16)
    middle = expand_pixels(tokens, half_deconv, half_bias).astype(jnp.bfloat16)
    coarse = lax.optimization_barrier(jnp.max(tokens.reshape(height // 2, 2, breadth // 2, 2, channels), axis=(1, 3)))
    sources = (finest, middle, tokens, coarse)
    return tuple((lateral(sources[number], laterals[number], level_gain[number, 0], level_shift[number, 0]) for number in range(4)))

def conv_three(padded, kernel):
    return lax.conv_general_dilated(padded[None], kernel, (1, 1), 'VALID', dimension_numbers=('NHWC', 'HWIO', 'NHWC'), preferred_element_type=jnp.float32)[0]

def flipped(kernel):
    return kernel[::-1, ::-1].transpose(0, 1, 3, 2)

def pad_grid(values):
    return jnp.pad(values, ((1, 1), (1, 1), (0, 0)))

def reference(features, attn_hidden, first_deconv, first_bias, mid_gain, mid_shift, second_deconv, second_bias, half_deconv, half_bias, lateral_four, lateral_eight, lateral_sixteen, lateral_coarse, output_conv, level_gain, level_shift, cotangent_four, cotangent_eight, cotangent_sixteen, cotangent_coarse):
    weights = (first_deconv, first_bias, mid_gain, mid_shift, second_deconv, second_bias, half_deconv, half_bias, (lateral_four, lateral_eight, lateral_sixteen, lateral_coarse), level_gain, level_shift)
    cotangents = (cotangent_four, cotangent_eight, cotangent_sixteen, cotangent_coarse)
    levels = [[], [], [], []]
    feature_grads = [None, None]
    for cascade_slot in range(2):
        image_index = 1 - cascade_slot
        tokens = features[image_index].reshape(H, W, D).astype(jnp.float32)
        lifted, pullback = jax.vjp(lambda values: lift_levels(values, weights), tokens)
        gradients = []
        for number in range(4):
            activated = lifted[number].astype(jnp.bfloat16)
            convolved = conv_three(pad_grid(activated), output_conv[number])
            normed, norm_pull = jax.vjp(lambda values: layer_norm(values, level_gain[number, 1], level_shift[number, 1]), convolved)
            levels[number].append(normed.astype(jnp.bfloat16))
            back_norm = norm_pull(cotangents[number][cascade_slot].astype(jnp.float32))[0].astype(jnp.bfloat16)
            gradients.append(conv_three(pad_grid(back_norm), flipped(output_conv[number])))
        feature_back = pullback(tuple(gradients))[0].astype(jnp.bfloat16)
        feature_grads[image_index] = feature_back.reshape(TOKENS, D)
    weight_grad = jnp.zeros((D, D), jnp.float32)
    for image_index in range(2):
        weight_grad = weight_grad + lax.dot_general(attn_hidden[image_index], feature_grads[image_index], (((0,), (0,)), ((), ())), preferred_element_type=jnp.float32)
    return (jnp.stack(levels[0]), jnp.stack(levels[1]), jnp.stack(levels[2]), jnp.stack(levels[3]), jnp.stack(feature_grads), weight_grad)
```

```python
import jax
import jax.numpy as jnp
import numpy as np
from jax import lax
from jax.experimental import pallas as pl
from jax.experimental.pallas import tpu as pltpu
from jax.sharding import PartitionSpec as P

EPS = 1e-06
F32 = jnp.float32
BF16 = jnp.bfloat16
MESH = pl.DeviceIdType.MESH

ROWS, COLS = 16, 8
OWN, RING = 128, 64
TOK = OWN + RING
DIRS = ((-1, 0), (1, 0), (0, -1), (0, 1), (-1, -1), (-1, 1), (1, -1), (1, 1))
OPPOSITE = (1, 0, 3, 2, 7, 6, 5, 4)


def token_index(r, c):
    if not (-1 <= r <= ROWS and -1 <= c <= COLS):
        return None
    if 0 <= r < ROWS and 0 <= c < COLS:
        return r * COLS + c
    if 0 <= c < COLS:
        return OWN + (0 if r < 0 else 8) + c
    if 0 <= r < ROWS:
        return OWN + (16 if c < 0 else 32) + r
    return OWN + 48 + (0 if r < 0 else 2) + (0 if c < 0 else 1)


TOKENS_AT = [(r, c) for r in range(-1, ROWS + 1) for c in range(-1, COLS + 1)]


def shift_matrices():
    out = np.zeros((3, 3, TOK, TOK), np.float32)
    for r, c in TOKENS_AT:
        for dy in range(-1, 2):
            for dx in range(-1, 2):
                there = token_index(r + dy, c + dx)
                if there is not None:
                    out[dy + 1, dx + 1, token_index(r, c), there] = 1
    return out


def ring_pick():
    out = np.zeros((RING, 128), np.float32)
    for c in range(8):
        out[c, 0 * 16 + 8 + c] = 1
        out[8 + c, 1 * 16 + c] = 1
    for r in range(16):
        out[16 + r, 2 * 16 + r] = 1
        out[32 + r, 3 * 16 + r] = 1
    out[48, 4 * 16 + 15] = 1
    out[49, 5 * 16 + 8] = 1
    out[50, 6 * 16 + 7] = 1
    out[51, 7 * 16 + 0] = 1
    return out


def column_pick():
    out = np.zeros((32, 128), np.float32)
    for r in range(16):
        out[r, r * 8] = 1
        out[16 + r, r * 8 + 7] = 1
    return out


SMALL_SIZE = (16, 16, 32, 32, 16, 16, 16, 16)
SMALL_AT = tuple(int(v) for v in np.cumsum((0,) + SMALL_SIZE)[:8])
SMALL = sum(SMALL_SIZE)


def edge_pixels(height, width, k):
    dy, dx = DIRS[k]
    rows = range(height) if dy == 0 else ([0] if dy < 0 else [height - 1])
    cols = range(width) if dx == 0 else ([0] if dx < 0 else [width - 1])
    return [(r, c) for r in rows for c in cols]


def small_send():
    out = np.zeros((SMALL, 160), np.float32)
    for k in range(8):
        at = SMALL_AT[k]
        for r, c in edge_pixels(16, 8, k):
            out[at, r * 8 + c] = 1
            at += 1
        for r, c in edge_pixels(8, 4, k):
            out[at, 128 + r * 4 + c] = 1
            at += 1
    return out


def halo_slot(height, width, r, c):
    k = DIRS.index(((r >= height) - (r < 0), (c >= width) - (c < 0)))
    return k, edge_pixels(height, width, OPPOSITE[k]).index((r % height, c % width))


def small_taps():
    out = np.zeros((9, 160, 160 + SMALL), np.float32)
    for base, height, width in ((0, 16, 8), (128, 8, 4)):
        for t in range(9):
            for r in range(height):
                for c in range(width):
                    rr, cc = r + t // 3 - 1, c + t % 3 - 1
                    if 0 <= rr < height and 0 <= cc < width:
                        out[t, base + r * width + c, base + rr * width + cc] = 1
                    else:
                        k, place = halo_slot(height, width, rr, cc)
                        place += len(edge_pixels(16, 8, OPPOSITE[k])) if base else 0
                        out[t, base + r * width + c, 160 + SMALL_AT[k] + place] = 1
    return out


COT_SIZE = (48, 48, 96, 96, 16, 16, 16, 16)
COT_AT = tuple(int(v) for v in np.cumsum((0,) + COT_SIZE)[:8])
COT = sum(COT_SIZE)


def cot_send():
    index = np.full((COT,), -1)
    for k in range(8):
        at = COT_AT[k]
        for r, c in edge_pixels(64, 32, k):
            index[at] = r * 32 + c
            at += 1
        for r, c in edge_pixels(32, 16, k):
            index[at] = 2048 + r * 16 + c
            at += 1
    return index


def cot_ring(n):
    height, width = ROWS * n, COLS * n
    out = np.zeros((n, n, RING, COT), np.float32)
    for r, c in TOKENS_AT:
        if 0 <= r < ROWS and 0 <= c < COLS:
            continue
        for ph in range(n):
            for pw in range(n):
                y, x = r * n + ph, c * n + pw
                if -1 <= y <= height and -1 <= x <= width:
                    k, place = halo_slot(height, width, y, x)
                    place += len(edge_pixels(64, 32, OPPOSITE[k])) if n == 2 else 0
                    out[ph, pw, token_index(r, c) - OWN, COT_AT[k] + place] = 1
    return out.reshape(n * n * RING, COT)


def interleave(n):
    tokens = 256 // n
    out = np.zeros((256, 256), np.float32)
    for t in range(tokens):
        for p in range(n):
            out[t * n + p, p * tokens + t] = 1
    return out


def quad_pick():
    out = np.zeros((4, 32, 128), np.float32)
    for q in range(4):
        for r in range(8):
            for c in range(4):
                out[q, r * 4 + c, (2 * r + q // 2) * 8 + 2 * c + q % 2] = 1
    return out


def chunk_split():
    out = np.zeros((320, 320), np.float32)
    for e in range(80):
        for p in range(4):
            out[p * 80 + e, e * 4 + p] = 1
    return out


def cot_pick():
    index = cot_send()
    out = np.zeros((COT, 2560), np.float32)
    for row, at in enumerate(index):
        if at >= 0:
            out[row, at] = 1
    return out


def const(array):
    return jnp.asarray(array, BF16)


def mm(a, b):
    return jnp.dot(a, b, preferred_element_type=F32)


def mt(a, b):
    return lax.dot_general(a, b, (((1,), (1,)), ((), ())), preferred_element_type=F32)


def pick(selection, a):
    return mm(selection, a).astype(BF16)


def normed(values):
    centre = jnp.mean(values, axis=-1, keepdims=True)
    values = values - centre
    scale = lax.rsqrt(jnp.mean(values * values, axis=-1, keepdims=True) + EPS)
    return values * scale, scale


def norm_back(unit, scale, grad):
    return scale * (
        grad
        - jnp.mean(grad, axis=-1, keepdims=True)
        - unit * jnp.mean(grad * unit, axis=-1, keepdims=True)
    )


def place():
    return lax.axis_index("segment"), lax.axis_index("tr"), lax.axis_index("tc")


def neighbour(k, s, tr, tc):
    dy, dx = DIRS[k]
    return (s, (tr + dy + 8) % 8, (tc + dx + 8) % 8)


def exists_mask(rows, spans):
    _, tr, tc = place()
    row = lax.broadcasted_iota(jnp.int32, (rows, 1), 0)
    mask = jnp.ones((rows, 1), F32)
    for k, lo, hi in spans:
        if k is None:
            there = 0.0
        else:
            dy, dx = DIRS[k]
            inside = (tr + dy >= 0) & (tr + dy < 8) & (tc + dx >= 0) & (tc + dx < 8)
            there = jnp.where(inside, 1.0, 0.0)
        mask = jnp.where((row >= lo) & (row < hi), there, mask)
    return mask


RING_SPANS = (
    (0, 128, 136), (1, 136, 144), (2, 144, 160), (3, 160, 176),
    (4, 176, 177), (5, 177, 178), (6, 178, 179), (7, 179, 180), (None, 180, 192),
)
SMALL_SPANS = tuple((k, SMALL_AT[k], SMALL_AT[k] + SMALL_SIZE[k]) for k in range(8))


def signal_all(peers):
    barrier = pltpu.get_barrier_semaphore()
    for peer in peers:
        pl.semaphore_signal(barrier, inc=1, device_id=peer, device_id_type=MESH)


def wait_all(peers):
    pl.semaphore_wait(pltpu.get_barrier_semaphore(), len(peers))


class Copies:
    def __init__(self, send, recv):
        self.send, self.recv, self.used, self.unsent = send, recv, 0, []

    def start(self, src, dst, peer):
        k, self.used = self.used, self.used + 1
        copy = pltpu.make_async_remote_copy(
            src_ref=src,
            dst_ref=dst,
            send_sem=self.send.at[k],
            recv_sem=self.recv.at[k],
            device_id=peer,
            device_id_type=MESH,
        )
        copy.start()
        self.unsent.append(copy)
        return copy

    def finish(self):
        for copy in self.unsent:
            copy.wait_send()


SPLIT = 1792


def split_product(row, weight):
    total = 0.0
    for _ in range(3):
        piece = row.astype(BF16)
        total = total + mm(piece, weight)
        row = row - piece.astype(F32)
    return total


def front_kernel(
    feat, attn, first, half, k2t, l4, l8, l16, lc, b2, bh, conv, gains, offsets, cot4, cot8, cot16, cotc,
    split, columns, ring_sel, edges, taps, quad, quad_t, cot_sel, cot_ring4, cot_ring8,
    wo, wr, xe, c2t, bias4, bias8, ring4, ring8, attn_t, dx_small, lev16, levc,
    w_own, w_rem, xa, aa, xt, at, xh, sides, small, small_h, back, back_h, cotm, cot_h, attn_c, attn_h, send, recv,
):
    s, tr, tc = place()
    other = 1 - s
    x_hi, y, z, core = tr // 4, tr % 4, tc // 2, tc % 2
    turn = 1 - 2 * core
    far = (other, (1 - x_hi) * 4 + y, tc)
    sibling = (s, tr, tc + turn)
    z_ahead = (s, tr, (z + turn + 4) % 4 * 2 + core)
    z_behind = (s, tr, (z - turn + 4) % 4 * 2 + core)
    y_ahead = (s, x_hi * 4 + (y + turn + 4) % 4, tc)
    y_behind = (s, x_hi * 4 + (y - turn + 4) % 4, tc)
    around = [neighbour(k, s, tr, tc) for k in range(8)]
    across = [(other, tr, (tc + o) % 8) for o in range(8)]
    along = [(s, tr, (tc + o) % 8) for o in range(1, 8)]
    peers = across + [far, sibling, z_ahead, z_behind, y_ahead, y_behind] + around + along
    signal_all(peers)
    copies = Copies(send, recv)

    def relayout(chunk):
        rows = pl.ds(pl.multiple_of(chunk * 80, 80), 80)
        block = mm(split[...], first[rows].reshape(320, 640)).astype(BF16)
        product = mm(half[rows].reshape(320, 640), l8[...]).astype(BF16)
        product = mm(split[...], product).astype(BF16)
        for p in range(4):
            w_own[chunk, :, 640 * p : 640 * p + 640] = block[80 * p : 80 * p + 80]
            w_own[chunk, :, 2560 + 256 * p : 2816 + 256 * p] = product[80 * p : 80 * p + 80]

    for j in range(8):
        for i in range(2):
            xa[j, 8 * i : 8 * i + 8] = feat[64 * i + 8 * j : 64 * i + 8 * j + 8]
            aa[j, 8 * i : 8 * i + 8] = attn[64 * i + 8 * j : 64 * i + 8 * j + 8]
    relayout(z)
    wait_all(peers)
    mine = pl.ds(pl.multiple_of(core * SPLIT, 128), SPLIT)
    x_copies = [copies.start(xa.at[(tc + o) % 8], xt.at[tc], across[o]) for o in range(8)]
    z_first = copies.start(w_own.at[z, :, mine], w_rem.at[z, :, mine], far)
    relayout(4 + y)
    y_first = copies.start(w_own.at[4 + y, :, mine], w_rem.at[4 + y, :, mine], far)
    pixels = jnp.concatenate([cot4[...].reshape(2048, 256), cot8[...].reshape(512, 256)])
    cotm[...] = pick(cot_sel[...], pixels)
    cot_copies = [
        copies.start(
            cotm.at[pl.ds(COT_AT[k], COT_SIZE[k])],
            cot_h.at[pl.ds(COT_AT[OPPOSITE[k]], COT_SIZE[k])],
            around[k],
        )
        for k in range(8)
    ]

    @pl.loop(1, 4)
    def rest(i):
        relayout((z + i) % 4)
        relayout(4 + (y + i) % 4)

    shared = []

    def share(chunk):
        shared.append(copies.start(w_rem.at[chunk, :, mine], w_rem.at[chunk, :, mine], sibling))

    for copy in x_copies:
        copy.wait_recv()
    x = xt[...].reshape(OWN, 1280)
    sides[...] = pick(columns[...], x).reshape(2, 16, 1280)
    sources = (xt.at[0], xt.at[7], sides.at[0], sides.at[1], xt.at[0], xt.at[0], xt.at[7], xt.at[7])
    halo_copies = [copies.start(sources[k], xh.at[OPPOSITE[k]], around[k]) for k in range(8)]
    quads = [pick(quad[q], x) for q in range(4)]
    coarse = jnp.maximum(jnp.maximum(quads[0], quads[1]), jnp.maximum(quads[2], quads[3]))
    units = [normed(mm(x, l16[...])), normed(mm(coarse, lc[...]))]
    laterals = jnp.concatenate(
        [(units[i][0] * gains[2 + i, 0:1] + offsets[2 + i, 0:1]).astype(BF16) for i in range(2)]
    )

    def exchange(rows, message, halo):
        message[...] = pick(edges[...], rows)
        return [
            copies.start(
                message.at[pl.ds(SMALL_AT[k], SMALL_SIZE[k])],
                halo.at[pl.ds(SMALL_AT[OPPOSITE[k]], SMALL_SIZE[k])],
                around[k],
            )
            for k in range(8)
        ]

    def small_conv(rows, halo, product, order):
        both = jnp.concatenate([rows, (halo[...] * exists_mask(SMALL, SMALL_SPANS)).astype(BF16)])
        sums = [jnp.zeros((128, 256), F32), jnp.zeros((32, 256), F32)]
        for t in range(9):
            moved = pick(taps[t], both)
            for i, (lo, hi) in enumerate(((0, 128), (128, 160))):
                sums[i] = sums[i] + product(moved[lo:hi], conv[2 + i, order(t)])
        return sums

    small_copies = exchange(laterals, small, small_h)
    z_first.wait_recv()
    z_up = copies.start(w_rem.at[z, :, mine], w_rem.at[z, :, mine], z_ahead)
    z_down = copies.start(w_rem.at[z, :, mine], w_rem.at[z, :, mine], z_behind)
    share(z)
    a_copies = [copies.start(aa.at[(tc + o) % 8], at.at[tc], across[o]) for o in range(8)]
    for p in range(4):
        c2t[p] = lax.dot_general(
            l4[...], k2t[p], (((0,), (0,)), ((), ())), preferred_element_type=F32
        ).astype(BF16)
    bias4[...] = split_product(b2[...], l4[...])
    bias8[...] = split_product(bh[...], l8[...])
    y_first.wait_recv()
    y_up = copies.start(w_rem.at[4 + y, :, mine], w_rem.at[4 + y, :, mine], y_ahead)
    y_down = copies.start(w_rem.at[4 + y, :, mine], w_rem.at[4 + y, :, mine], y_behind)
    share(4 + y)
    for copy in small_copies:
        copy.wait_recv()
    sums = small_conv(laterals, small_h, mm, lambda t: t)
    grads = []
    for i, (cot, level_out) in enumerate(((cot16, lev16), (cotc, levc))):
        unit, scale = normed(sums[i])
        gain = gains[2 + i, 1:2]
        level_out[...] = (unit * gain + offsets[2 + i, 1:2]).astype(BF16)
        grads.append(norm_back(unit, scale, cot[...].astype(F32) * gain).astype(BF16))
    grads = jnp.concatenate(grads)
    back_copies = exchange(grads, back, back_h)

    z_ring = [(z - turn + 4) % 4, (z + turn + 4) % 4, (z + 2) % 4]
    y_ring = [4 + (y - turn + 4) % 4, 4 + (y + turn + 4) % 4, 4 + (y + 2) % 4]
    z_up.wait_recv()
    z_on = copies.start(w_rem.at[z_ring[0], :, mine], w_rem.at[z_ring[0], :, mine], z_ahead)
    share(z_ring[0])
    z_down.wait_recv()
    share(z_ring[1])
    y_up.wait_recv()
    y_on = copies.start(w_rem.at[y_ring[0], :, mine], w_rem.at[y_ring[0], :, mine], y_ahead)
    share(y_ring[0])
    y_down.wait_recv()
    share(y_ring[1])

    for copy in a_copies:
        copy.wait_recv()
    tile = at[...].reshape(OWN, 1280)
    row = lax.broadcasted_iota(jnp.int32, (1280, 256), 0)
    column = lax.broadcasted_iota(jnp.int32, (1280, 256), 1)
    row = jnp.where(column % 16 < 10, row - column // 16 * 80 - column % 16, -1)

    @pl.loop(0, 8)
    def attn_columns(j):
        attn_c[j] = mm(tile, (row == 10 * j).astype(F32).astype(BF16)).astype(BF16)

    attn_copies = [
        copies.start(attn_c.at[(tc + o) % 8], attn_h.at[tc], along[o - 1]) for o in range(1, 8)
    ]
    attn_h[tc] = attn_c[tc]

    for copy in back_copies:
        copy.wait_recv()
    sums = small_conv(grads, back_h, mt, lambda t: 8 - t)
    steps = []
    for i, weight in enumerate((l16, lc)):
        unit, scale = units[i]
        steps.append(mt(norm_back(unit, scale, sums[i] * gains[2 + i, 0:1]).astype(BF16), weight[...]))
    hits = [jnp.where(q.astype(F32) == coarse.astype(F32), 1.0, 0.0) for q in quads]
    portion = steps[1] / (hits[0] + hits[1] + hits[2] + hits[3])
    total = steps[0]
    for q in range(4):
        total = total + mm(quad_t[q], (hits[q] * portion).astype(BF16))
    dx_small[...] = total

    for copy in halo_copies + cot_copies:
        copy.wait_recv()
    xe[:OWN] = x
    xe[OWN:] = pick(ring_sel[...], xh[...].reshape(128, 1280))
    ring4[...] = pick(cot_ring4[...], cot_h[...]).reshape(4, 4, RING, 256)
    ring8[...] = pick(cot_ring8[...], cot_h[...]).reshape(2, 2, RING, 256)
    wo[...] = w_own[...]
    z_on.wait_recv()
    share(z_ring[2])
    y_on.wait_recv()
    share(y_ring[2])
    for copy in attn_copies:
        copy.wait_recv()
    for j in range(8):
        attn_t[:, 128 * j : 128 * j + 128] = attn_h[j].T
    for copy in shared:
        copy.wait_recv()
    wr[...] = w_rem[...]
    copies.finish()


def shape(dims, dtype=BF16):
    return jax.ShapeDtypeStruct(dims, dtype)


def call(kernel, outs, scratch, args, collective_id=None):
    vmem = pl.BlockSpec(memory_space=pltpu.VMEM)
    params = {"vmem_limit_bytes": 60 * 2**20}
    if collective_id is not None:
        params.update(collective_id=collective_id, has_side_effects=True)
    return pl.pallas_call(
        kernel,
        out_shape=outs,
        in_specs=[vmem] * len(args),
        out_specs=[vmem] * len(outs),
        scratch_shapes=scratch,
        compiler_params=pltpu.CompilerParams(**params),
    )(*args)


def buffer(*dims):
    return pltpu.VMEM(dims, BF16)


def front(*args):
    copies = 8 + 2 + 8 + 8 + 8 + 4 + 8 + 8 + 8 + 2 + 7
    return call(
        front_kernel,
        [
            shape((8, 80, 3584)), shape((8, 80, 3584)), shape((TOK, 1280)), shape((4, 256, 640)),
            shape((1, 256), F32), shape((1, 256), F32), shape((4, 4, RING, 256)), shape((2, 2, RING, 256)),
            shape((256, 1024)), shape((OWN, 1280), F32), shape((128, 256)), shape((32, 256)),
        ],
        [
            buffer(8, 80, 3584), buffer(8, 80, 3584),
            buffer(8, 16, 1280), buffer(8, 16, 1280), buffer(8, 16, 1280), buffer(8, 16, 1280),
            buffer(8, 16, 1280), buffer(2, 16, 1280),
            buffer(SMALL, 256), buffer(SMALL, 256), buffer(SMALL, 256), buffer(SMALL, 256),
            buffer(COT, 256), buffer(COT, 256), buffer(8, OWN, 256), buffer(8, OWN, 256),
            pltpu.SemaphoreType.DMA((copies,)), pltpu.SemaphoreType.DMA((copies,)),
        ],
        args,
        collective_id=0,
    )


def erf(x):
    x = jnp.clip(x, -3.832506856900711, 3.832506856900711)
    square = x * x
    over = jnp.full_like(x, 0.00022905065861350646)
    for c in (0.0034082910107109506, 0.050955695062380861, 0.18520832239976145, 1.128379143519084):
        over = over * square + c
    under = jnp.full_like(x, -1.1791602954361697e-7)
    for c in (0.000023547966471313185, 0.0010179625278914885, 0.014070470171167667,
              0.11098505178285362, 0.49746925110067538, 1.0):
        under = under * square + c
    return x * over / under


def fill_shifted(padded, n, shifts):
    for i in range(n + 2):
        for j in range(n + 2):
            dy, dx = (i - 1) // n, (j - 1) // n
            if dy or dx:
                source = padded[(i - 1) % n + 1, (j - 1) % n + 1]
                padded[i, j] = mm(shifts[3 * dy + dx + 4], source).astype(BF16)


def pyramid_level(n, lat, back, unit, scale, conv, cot, ring, out, gains, offsets, keep, shifts, split, done):
    groups = n * n // 8 if n == 4 else 1
    rows = ROWS // groups
    fill_shifted(lat, n, shifts)

    @pl.loop(0, n)
    def forward(ph):
        acc = jnp.zeros((n * TOK, 256), F32)
        for t in range(9):
            dy, dx = t // 3, t % 3
            block = lat[ph + dy, dx : dx + n].reshape(n * TOK, 256)
            acc = acc + mm(block, conv[t])
        pieces = []
        for g in range(groups):
            block = cot[pl.ds(rows * g, rows), ph].reshape(256, 256)
            pieces.append(mm(split[1], block))
        tokens = 256 // n
        results = []
        for pw in range(n):
            values, size = normed(acc[pw * TOK : pw * TOK + TOK])
            results.append((values[:OWN] * gains[1:2] + offsets[1:2]).astype(BF16))
            own = [piece[pw * tokens : pw * tokens + tokens] for piece in pieces]
            grads = jnp.concatenate(own + [ring[ph, pw].astype(F32)], axis=0)
            grads = norm_back(values, size, grads * gains[1:2])
            back[ph + 1, pw + 1] = (grads * keep).astype(BF16)
        for g in range(groups):
            block = jnp.concatenate([r[g * tokens : g * tokens + tokens] for r in results], axis=0)
            block = mm(split[0], block).astype(BF16)
            out[pl.ds(rows * g, rows), ph] = block.reshape(rows, 8 * n, 256)

    fill_shifted(back, n, shifts)

    @pl.loop(0, n)
    def backward(ph):
        acc = jnp.zeros((n * OWN, 256), F32)
        for t in range(9):
            dy, dx = t // 3, t % 3
            block = jnp.concatenate([back[ph + dy, dx + pw, :OWN] for pw in range(n)], axis=0)
            acc = acc + mt(block, conv[8 - t])
        for pw in range(n):
            grads = acc[pw * OWN : pw * OWN + OWN] * gains[0:1]
            done(ph, pw, norm_back(unit[ph, pw], scale[ph, pw], grads).astype(BF16))


def levels_kernel(
    xe, wo, wr, second, conv, cot4, cot8, ring4, ring8, dx_small, shifts, split4, split8,
    bias1, gain_m, shift_m, bias4, bias8, gains, offsets,
    out4, out8, dx,
    up, unit_u, slope_u, scale_u, lat4, back4, unit4, scale4, lat8, back8, unit8, scale8, d4, dfull,
):
    keep = exists_mask(TOK, RING_SPANS)
    s, _, _ = place()
    own = pl.ds(pl.multiple_of(640 * s, 128), 640)
    other = pl.ds(pl.multiple_of(640 - 640 * s, 128), 640)
    xo, xr = xe[:, own], xe[:, other]
    for p in range(4):
        cols = pl.ds(640 * p, 640)
        pre = mm(xo, wo[:, cols]) + mm(xr, wr[:, cols]) + bias1[...]
        unit, size = normed(pre)
        before = unit * gain_m[...] + shift_m[...]
        cdf = 0.5 * (1 + erf(before * (0.5**0.5)))
        up[p] = (before * cdf).astype(BF16)
        inner = before[:OWN]
        unit_u[p] = unit[:OWN]
        scale_u[p] = size[:OWN]
        slope_u[p] = (cdf[:OWN] + inner * jnp.exp(-0.5 * inner * inner) * (1 / np.sqrt(2 * np.pi))) * gain_m[...]
    for p in range(4):
        for q in range(4):
            ph, pw = 2 * (p // 2) + q // 2, 2 * (p % 2) + q % 2
            pre = mt(up[p], second[q]) + bias4[...]
            unit, size = normed(pre)
            unit4[ph, pw] = unit[:OWN]
            scale4[ph, pw] = size[:OWN]
            lat4[ph + 1, pw + 1] = ((unit * gains[0, 0:1] + offsets[0, 0:1]) * keep).astype(BF16)
    for p in range(4):
        cols = pl.ds(2560 + 256 * p, 256)
        pre = mm(xo, wo[:, cols]) + mm(xr, wr[:, cols]) + bias8[...]
        unit, size = normed(pre)
        unit8[p // 2, p % 2] = unit[:OWN]
        scale8[p // 2, p % 2] = size[:OWN]
        lat8[p // 2 + 1, p % 2 + 1] = ((unit * gains[1, 0:1] + offsets[1, 0:1]) * keep).astype(BF16)

    def done4(ph, pw, grads):
        d4[2 * (ph // 2) + pw // 2, 2 * (ph % 2) + pw % 2] = grads

    def done8(ph, pw, grads):
        d8[2 * ph + pw] = grads

    d8 = d4.at[4]
    pyramid_level(
        4, lat4, back4, unit4, scale4, conv.at[0], cot4, ring4, out4, gains[0], offsets[0], keep, shifts, split4, done4
    )
    pyramid_level(
        2, lat8, back8, unit8, scale8, conv.at[1], cot8, ring8, out8, gains[1], offsets[1], keep, shifts, split8, done8
    )
    dup = jnp.zeros((4 * OWN, 640), F32)
    for q in range(4):
        block = jnp.concatenate([d4[p, q] for p in range(4)], axis=0)
        dup = dup + mm(block, second[q])
    for p in range(4):
        grads = norm_back(unit_u[p], scale_u[p], dup[p * OWN : p * OWN + OWN] * slope_u[p])
        dfull[:, 640 * p : 640 * p + 640] = grads.astype(BF16)
        dfull[:, 2560 + 256 * p : 2816 + 256 * p] = d4[4, p]
    dx[:, own] = (mt(dfull[...], wo[...]) + dx_small[:, own]).astype(BF16)
    dx[:, other] = (mt(dfull[...], wr[...]) + dx_small[:, other]).astype(BF16)


def levels(*args):
    def wide(*dims):
        return pltpu.VMEM(dims, F32)

    return call(
        levels_kernel,
        [shape((16, 4, 32, 256)), shape((16, 2, 16, 256)), shape((OWN, 1280))],
        [
            buffer(4, TOK, 640), wide(4, OWN, 640), wide(4, OWN, 640), wide(4, OWN, 1),
            buffer(6, 6, TOK, 256), buffer(6, 6, TOK, 256), wide(4, 4, OWN, 256), wide(4, 4, OWN, 1),
            buffer(4, 4, TOK, 256), buffer(4, 4, TOK, 256), wide(2, 2, OWN, 256), wide(2, 2, OWN, 1),
            buffer(5, 4, OWN, 256), buffer(OWN, 3584),
        ],
        args,
    )


def last_kernel(dx, attn_t, grads, weight, mine, home, tiles, part, parts, send, recv):
    s, tr, tc = place()
    other, me = 1 - s, s * 8 + tr
    sibling = (s, tr, tc + 1 - 2 * (tc % 2))
    ring = [(s, tr, (tc + 2 * j) % 8) for j in (1, 3, 2)]
    across = [(other, tr, (tc + o) % 8) for o in range(8)]
    plane = [((me + o) % 16 // 8, (me + o) % 8, tc) for o in range(1, 16)]
    peers = across + ring + [sibling] + plane
    signal_all(peers)
    copies = Copies(send, recv)
    mine[...] = dx[...].reshape(8, 16, 1280)
    wait_all(peers)
    received = [copies.start(mine, tiles.at[tc], peer) for peer in ring]
    shared = [copies.start(mine, tiles.at[tc], sibling)]
    homes = [copies.start(mine.at[(tc + o) % 8], home.at[tc], across[o]) for o in range(8)]
    tiles[tc] = mine[...]
    for copy, j in zip(received, (1, 3, 2)):
        copy.wait_recv()
        slot = (tc + 8 - 2 * j) % 8
        shared.append(copies.start(tiles.at[slot], tiles.at[slot], sibling))
    for copy in shared:
        copy.wait_recv()
    product = mm(attn_t[...], tiles[...].reshape(8 * OWN, 1280))
    part[...] = product.astype(BF16).reshape(16, 16, 1280)
    sums = [copies.start(part.at[(me + o) % 16], parts.at[me], plane[o - 1]) for o in range(1, 16)]
    parts[me] = part[me]
    for copy in homes:
        copy.wait_recv()
    for j in range(8):
        for i in range(2):
            grads[64 * i + 8 * j : 64 * i + 8 * j + 8] = home[j, 8 * i : 8 * i + 8]
    for copy in sums:
        copy.wait_recv()
    total = parts[0].astype(F32)
    for j in range(1, 16):
        total = total + parts[j].astype(F32)
    weight[...] = total[:10]
    copies.finish()


def last(*args):
    copies = 3 + 1 + 8 + 3 + 15
    return call(
        last_kernel,
        [shape((OWN, 1280)), shape((10, 1280), F32)],
        [
            buffer(8, 16, 1280), buffer(8, 16, 1280), buffer(8, 8, 16, 1280),
            buffer(16, 16, 1280), buffer(16, 16, 1280),
            pltpu.SemaphoreType.DMA((copies,)), pltpu.SemaphoreType.DMA((copies,)),
        ],
        args,
        collective_id=1,
    )


def body(
    features,
    attn_hidden,
    first_deconv,
    first_bias,
    mid_gain,
    mid_shift,
    second_deconv,
    second_bias,
    half_deconv,
    half_bias,
    lateral_four,
    lateral_eight,
    lateral_sixteen,
    lateral_coarse,
    output_conv,
    level_gain,
    level_shift,
    cotangent_four,
    cotangent_eight,
    cotangent_sixteen,
    cotangent_coarse,
):
    k2t = second_deconv.transpose(1, 2, 3, 0).reshape(4, 320, 640)
    conv = output_conv.reshape(4, 9, 256, 256)
    cot4 = cotangent_four.reshape(16, 4, 32, 256)
    cot8 = cotangent_eight.reshape(16, 2, 16, 256)
    quads = quad_pick()
    rings = cot_ring(4), cot_ring(2)
    wo, wr, xe, c2t, bias4, bias8, ring4, ring8, attn_t, dx_small, lev16, levc = front(
        features[0], attn_hidden[0], first_deconv, half_deconv, k2t,
        lateral_four, lateral_eight, lateral_sixteen, lateral_coarse,
        second_bias.reshape(1, 320), half_bias.reshape(1, 640),
        conv, level_gain, level_shift, cot4, cot8,
        cotangent_sixteen.reshape(128, 256), cotangent_coarse.reshape(32, 256),
        const(chunk_split()), const(column_pick()), const(ring_pick()), const(small_send()),
        const(small_taps()), const(quads), const(quads.transpose(0, 2, 1)), const(cot_pick()),
        const(rings[0]), const(rings[1]),
    )
    split4, split8 = (const(np.stack([interleave(n), interleave(n).T])) for n in (4, 2))
    out4, out8, dx = levels(
        xe, wo.reshape(640, 3584), wr.reshape(640, 3584), c2t, conv, cot4, cot8, ring4, ring8, dx_small,
        const(shift_matrices().reshape(9, TOK, TOK)), split4, split8,
        first_bias.reshape(1, 640), mid_gain.reshape(1, 640), mid_shift.reshape(1, 640),
        bias4, bias8, level_gain, level_shift,
    )
    grads, weight = last(dx, attn_t)
    return (
        out4.reshape(1, 64, 32, 256),
        out8.reshape(1, 32, 16, 256),
        lev16.reshape(1, 16, 8, 256),
        levc.reshape(1, 8, 4, 256),
        grads[None],
        weight,
    )


def solution(mesh):
    tokens = P("segment", ("tr", "tc"), None)
    deconv = P("segment", None, None, None)
    grid = P("segment", "tr", "tc", None)
    placed = (
        (tokens, tokens, deconv) + (P(),) * 5 + (deconv,) + (P(),) * 8 + (grid,) * 4
    )
    return jax.shard_map(
        body,
        mesh=mesh,
        in_specs=placed,
        out_specs=(grid, grid, grid, grid, tokens, P(("segment", "tr", "tc"), None)),
        check_vma=False,
    )
```

```python
import jax
import jax.numpy as jnp
import numpy as np
from jax import lax
from jax.experimental import pallas as pl
from jax.experimental.pallas import tpu as pltpu
from jax.sharding import PartitionSpec as P

EPS = 1e-06
F32 = jnp.float32
BF16 = jnp.bfloat16
MESH = pl.DeviceIdType.MESH

ROWS, COLS = 16, 8
OWN, RING = 128, 64
TOK = OWN + RING
DIRS = ((-1, 0), (1, 0), (0, -1), (0, 1), (-1, -1), (-1, 1), (1, -1), (1, 1))
OPPOSITE = (1, 0, 3, 2, 7, 6, 5, 4)


def token_index(r, c):
    if not (-1 <= r <= ROWS and -1 <= c <= COLS):
        return None
    if 0 <= r < ROWS and 0 <= c < COLS:
        return r * COLS + c
    if 0 <= c < COLS:
        return OWN + (0 if r < 0 else 8) + c
    if 0 <= r < ROWS:
        return OWN + (16 if c < 0 else 32) + r
    return OWN + 48 + (0 if r < 0 else 2) + (0 if c < 0 else 1)


TOKENS_AT = [(r, c) for r in range(-1, ROWS + 1) for c in range(-1, COLS + 1)]


def shift_matrices():
    out = np.zeros((3, 3, TOK, TOK), np.float32)
    for r, c in TOKENS_AT:
        for dy in range(-1, 2):
            for dx in range(-1, 2):
                there = token_index(r + dy, c + dx)
                if there is not None:
                    out[dy + 1, dx + 1, token_index(r, c), there] = 1
    return out


def ring_pick():
    out = np.zeros((RING, 128), np.float32)
    for c in range(8):
        out[c, 0 * 16 + 8 + c] = 1
        out[8 + c, 1 * 16 + c] = 1
    for r in range(16):
        out[16 + r, 2 * 16 + r] = 1
        out[32 + r, 3 * 16 + r] = 1
    out[48, 4 * 16 + 15] = 1
    out[49, 5 * 16 + 8] = 1
    out[50, 6 * 16 + 7] = 1
    out[51, 7 * 16 + 0] = 1
    return out


def column_pick():
    out = np.zeros((32, 128), np.float32)
    for r in range(16):
        out[r, r * 8] = 1
        out[16 + r, r * 8 + 7] = 1
    return out


SMALL_SIZE = (16, 16, 32, 32, 16, 16, 16, 16)
SMALL_AT = tuple(int(v) for v in np.cumsum((0,) + SMALL_SIZE)[:8])
SMALL = sum(SMALL_SIZE)


def edge_pixels(height, width, k):
    dy, dx = DIRS[k]
    rows = range(height) if dy == 0 else ([0] if dy < 0 else [height - 1])
    cols = range(width) if dx == 0 else ([0] if dx < 0 else [width - 1])
    return [(r, c) for r in rows for c in cols]


def small_send():
    out = np.zeros((SMALL, 160), np.float32)
    for k in range(8):
        at = SMALL_AT[k]
        for r, c in edge_pixels(16, 8, k):
            out[at, r * 8 + c] = 1
            at += 1
        for r, c in edge_pixels(8, 4, k):
            out[at, 128 + r * 4 + c] = 1
            at += 1
    return out


def halo_slot(height, width, r, c):
    k = DIRS.index(((r >= height) - (r < 0), (c >= width) - (c < 0)))
    return k, edge_pixels(height, width, OPPOSITE[k]).index((r % height, c % width))


def small_taps():
    out = np.zeros((9, 160, 160 + SMALL), np.float32)
    for base, height, width in ((0, 16, 8), (128, 8, 4)):
        for t in range(9):
            for r in range(height):
                for c in range(width):
                    rr, cc = r + t // 3 - 1, c + t % 3 - 1
                    if 0 <= rr < height and 0 <= cc < width:
                        out[t, base + r * width + c, base + rr * width + cc] = 1
                    else:
                        k, place = halo_slot(height, width, rr, cc)
                        place += len(edge_pixels(16, 8, OPPOSITE[k])) if base else 0
                        out[t, base + r * width + c, 160 + SMALL_AT[k] + place] = 1
    return out


COT_SIZE = (48, 48, 96, 96, 16, 16, 16, 16)
COT_AT = tuple(int(v) for v in np.cumsum((0,) + COT_SIZE)[:8])
COT = sum(COT_SIZE)


def cot_send():
    index = np.full((COT,), -1)
    for k in range(8):
        at = COT_AT[k]
        for r, c in edge_pixels(64, 32, k):
            index[at] = r * 32 + c
            at += 1
        for r, c in edge_pixels(32, 16, k):
            index[at] = 2048 + r * 16 + c
            at += 1
    return index


def cot_ring(n):
    height, width = ROWS * n, COLS * n
    out = np.zeros((n, n, RING, COT), np.float32)
    for r, c in TOKENS_AT:
        if 0 <= r < ROWS and 0 <= c < COLS:
            continue
        for ph in range(n):
            for pw in range(n):
                y, x = r * n + ph, c * n + pw
                if -1 <= y <= height and -1 <= x <= width:
                    k, place = halo_slot(height, width, y, x)
                    place += len(edge_pixels(64, 32, OPPOSITE[k])) if n == 2 else 0
                    out[ph, pw, token_index(r, c) - OWN, COT_AT[k] + place] = 1
    return out.reshape(n * n * RING, COT)


def interleave(n):
    tokens = 256 // n
    out = np.zeros((256, 256), np.float32)
    for t in range(tokens):
        for p in range(n):
            out[t * n + p, p * tokens + t] = 1
    return out


def quad_pick():
    out = np.zeros((4, 32, 128), np.float32)
    for q in range(4):
        for r in range(8):
            for c in range(4):
                out[q, r * 4 + c, (2 * r + q // 2) * 8 + 2 * c + q % 2] = 1
    return out


def chunk_split():
    out = np.zeros((320, 320), np.float32)
    for e in range(80):
        for p in range(4):
            out[p * 80 + e, e * 4 + p] = 1
    return out


def cot_pick():
    index = cot_send()
    out = np.zeros((COT, 2560), np.float32)
    for row, at in enumerate(index):
        if at >= 0:
            out[row, at] = 1
    return out


def const(array):
    return jnp.asarray(array, BF16)


def mm(a, b):
    return jnp.dot(a, b, preferred_element_type=F32)


def mt(a, b):
    return lax.dot_general(a, b, (((1,), (1,)), ((), ())), preferred_element_type=F32)


def pick(selection, a):
    return mm(selection, a).astype(BF16)


def normed(values):
    centre = jnp.mean(values, axis=-1, keepdims=True)
    values = values - centre
    scale = lax.rsqrt(jnp.mean(values * values, axis=-1, keepdims=True) + EPS)
    return values * scale, scale


def norm_back(unit, scale, grad):
    return scale * (
        grad
        - jnp.mean(grad, axis=-1, keepdims=True)
        - unit * jnp.mean(grad * unit, axis=-1, keepdims=True)
    )


def place():
    return lax.axis_index("segment"), lax.axis_index("tr"), lax.axis_index("tc")


def neighbour(k, s, tr, tc):
    dy, dx = DIRS[k]
    return (s, (tr + dy + 8) % 8, (tc + dx + 8) % 8)


def exists_mask(rows, spans):
    _, tr, tc = place()
    row = lax.broadcasted_iota(jnp.int32, (rows, 1), 0)
    mask = jnp.ones((rows, 1), F32)
    for k, lo, hi in spans:
        if k is None:
            there = 0.0
        else:
            dy, dx = DIRS[k]
            inside = (tr + dy >= 0) & (tr + dy < 8) & (tc + dx >= 0) & (tc + dx < 8)
            there = jnp.where(inside, 1.0, 0.0)
        mask = jnp.where((row >= lo) & (row < hi), there, mask)
    return mask


RING_SPANS = (
    (0, 128, 136), (1, 136, 144), (2, 144, 160), (3, 160, 176),
    (4, 176, 177), (5, 177, 178), (6, 178, 179), (7, 179, 180), (None, 180, 192),
)
SMALL_SPANS = tuple((k, SMALL_AT[k], SMALL_AT[k] + SMALL_SIZE[k]) for k in range(8))


def signal_all(peers):
    barrier = pltpu.get_barrier_semaphore()
    for peer in peers:
        pl.semaphore_signal(barrier, inc=1, device_id=peer, device_id_type=MESH)


def wait_all(peers):
    pl.semaphore_wait(pltpu.get_barrier_semaphore(), len(peers))


class Copies:
    def __init__(self, send, recv):
        self.send, self.recv, self.used, self.unsent = send, recv, 0, []

    def start(self, src, dst, peer):
        k, self.used = self.used, self.used + 1
        copy = pltpu.make_async_remote_copy(
            src_ref=src,
            dst_ref=dst,
            send_sem=self.send.at[k],
            recv_sem=self.recv.at[k],
            device_id=peer,
            device_id_type=MESH,
        )
        copy.start()
        self.unsent.append(copy)
        return copy

    def finish(self):
        for copy in self.unsent:
            copy.wait_send()


SPLIT = 896


def split_product(row, weight):
    total = 0.0
    for _ in range(3):
        piece = row.astype(BF16)
        total = total + mm(piece, weight)
        row = row - piece.astype(F32)
    return total


def main_kernel(
    feat, attn, first, half, k2t, l4, l8, l16, lc, b2, bh, conv, gains, offsets, cot4, cot8, cot16, cotc,
    split, columns, ring_sel, edges, taps, quad, quad_t, cot_sel, cot_ring4, cot_ring8,
    shifts, split4, split8, bias1, gain_m, shift_m,
    out4, out8, lev16, levc, home_out, parts_out,
    w, first_v, half_v, xa, aa, xt, at, xh, sides, small, small_h, back_s, back_h, cotm, cot_h, attn_c, attn_h,
    xe, c2t, ring4, ring8, dx_small, up, unit_u, slope_u, scale_u, lat, back, unit_l, scale_l, d4, dfull,
    attn_t, mine, home, tiles, part, parts, send, recv, load,
):
    s, tr, tc = place()
    other = 1 - s
    x_hi, y, z, core = tr // 4, tr % 4, tc // 2, tc % 2
    turn = 1 - 2 * core
    far = (other, (1 - x_hi) * 4 + y, tc)
    balance = (other, (1 - x_hi + core * (2 * x_hi - 1)) * 4 + y, tc)
    sibling = (s, tr, tc + turn)
    z_ahead = (s, tr, (z + turn + 4) % 4 * 2 + core)
    z_behind = (s, tr, (z - turn + 4) % 4 * 2 + core)
    y_ahead = (s, x_hi * 4 + (y + turn + 4) % 4, tc)
    y_behind = (s, x_hi * 4 + (y - turn + 4) % 4, tc)
    around = [neighbour(k, s, tr, tc) for k in range(8)]
    across = [(other, tr, (tc + o) % 8) for o in range(8)]
    along = [(s, tr, (tc + o) % 8) for o in range(1, 8)]
    me = s * 8 + tr
    plane = [((me + o) % 16 // 8, (me + o) % 8, tc) for o in range(1, 16)]
    peers = plane + across + [far, balance, sibling, z_ahead, z_behind, y_ahead, y_behind] + around + along
    signal_all(peers)
    copies = Copies(send, recv)

    def chunk_at(i):
        return i % 2 * 4 + (jnp.where(i % 2 == 0, z, y) + i // 2) % 4

    def loads(slot):
        rows = pl.ds(chunk_at(order[slot]) * 80, 80)
        return [
            pltpu.make_async_copy(ref.at[rows], slots.at[slot], load.at[k, slot])
            for k, (ref, slots) in enumerate(((first, first_v), (half, half_v)))
        ]

    def relayout(slot):
        for copy in loads(slot):
            copy.wait()
        block = mm(split[...], first_v[slot].reshape(320, 640)).astype(BF16)
        product = mm(half_v[slot].reshape(320, 640), l8[...]).astype(BF16)
        product = mm(split[...], product).astype(BF16)
        rows = pl.ds(pl.multiple_of(640 * s + chunk_at(order[slot]) * 80, 16), 80)
        for p in range(4):
            w[rows, 640 * p : 640 * p + 640] = block[80 * p : 80 * p + 80]
            w[rows, 2560 + 256 * p : 2816 + 256 * p] = product[80 * p : 80 * p + 80]
        return w.at[rows]

    order = [0, 1, 2 + core, 4 + core, 6 + core]

    def piece(owner, chunk, h):
        rows = pl.ds(pl.multiple_of(640 * owner + chunk * 80, 16), 80)
        return w.at[rows, pl.ds(pl.multiple_of(core * 2 * SPLIT + h * SPLIT, 128), SPLIT)]

    def send_pieces(chunk, peer):
        return [copies.start(piece(s, chunk, h), piece(s, chunk, h), peer) for h in range(2)]

    shared = []

    def pass_on(arrived, chunk, peers):
        sent = [[] for _ in peers]
        for h, copy in enumerate(arrived):
            copy.wait_recv()
            part = piece(other, chunk, h)
            for onward, peer in zip(sent, peers):
                onward.append(copies.start(part, part, peer))
            shared.append(copies.start(part, part, sibling))
        return sent

    for slot in range(5):
        for copy in loads(slot):
            copy.start()
    for j in range(8):
        for i in range(2):
            xa[j, 8 * i : 8 * i + 8] = feat[64 * i + 8 * j : 64 * i + 8 * j + 8]
            aa[j, 8 * i : 8 * i + 8] = attn[64 * i + 8 * j : 64 * i + 8 * j + 8]
    relayout(0)
    wait_all(peers)
    x_copies = [copies.start(xa.at[(tc + o) % 8], xt.at[tc], across[o]) for o in range(8)]
    z_first = send_pieces(z, far)
    relayout(1)
    y_first = send_pieces(4 + y, balance)
    pixels = jnp.concatenate([cot4[...].reshape(2048, 256), cot8[...].reshape(512, 256)])
    cotm[...] = pick(cot_sel[...], pixels)
    cot_copies = [
        copies.start(
            cotm.at[pl.ds(COT_AT[k], COT_SIZE[k])],
            cot_h.at[pl.ds(COT_AT[OPPOSITE[k]], COT_SIZE[k])],
            around[k],
        )
        for k in range(8)
    ]

    for slot in range(2, 5):
        rows = relayout(slot)
        shared.append(copies.start(rows, rows, sibling))
    z_up, z_down = pass_on(z_first, z, [z_ahead, z_behind])

    for copy in x_copies:
        copy.wait_recv()
    x = xt[...].reshape(OWN, 1280)
    sides[...] = pick(columns[...], x).reshape(2, 16, 1280)
    sources = (xt.at[0], xt.at[7], sides.at[0], sides.at[1], xt.at[0], xt.at[0], xt.at[7], xt.at[7])
    halo_copies = [copies.start(sources[k], xh.at[OPPOSITE[k]], around[k]) for k in range(8)]
    quads = [pick(quad[q], x) for q in range(4)]
    coarse = jnp.maximum(jnp.maximum(quads[0], quads[1]), jnp.maximum(quads[2], quads[3]))
    units = [normed(mm(x, l16[...])), normed(mm(coarse, lc[...]))]
    laterals = jnp.concatenate(
        [(units[i][0] * gains[2 + i, 0:1] + offsets[2 + i, 0:1]).astype(BF16) for i in range(2)]
    )

    def exchange(rows, message, halo):
        message[...] = pick(edges[...], rows)
        return [
            copies.start(
                message.at[pl.ds(SMALL_AT[k], SMALL_SIZE[k])],
                halo.at[pl.ds(SMALL_AT[OPPOSITE[k]], SMALL_SIZE[k])],
                around[k],
            )
            for k in range(8)
        ]

    def small_conv(rows, halo, product, order):
        both = jnp.concatenate([rows, (halo[...] * exists_mask(SMALL, SMALL_SPANS)).astype(BF16)])
        sums = [jnp.zeros((128, 256), F32), jnp.zeros((32, 256), F32)]
        for t in range(9):
            moved = pick(taps[t], both)
            for i, (lo, hi) in enumerate(((0, 128), (128, 160))):
                sums[i] = sums[i] + product(moved[lo:hi], conv[2 + i, order(t)])
        return sums

    small_copies = exchange(laterals, small, small_h)
    for p in range(4):
        c2t[p] = lax.dot_general(
            l4[...], k2t[p], (((0,), (0,)), ((), ())), preferred_element_type=F32
        ).astype(BF16)
    bias4 = split_product(b2[...].reshape(1, 320), l4[...])
    bias8 = split_product(bh[...].reshape(1, 640), l8[...])
    y_up, y_down = pass_on(y_first, 4 + y, [y_ahead, y_behind])
    a_copies = [copies.start(aa.at[(tc + o) % 8], at.at[tc], across[o]) for o in range(8)]
    for copy in small_copies:
        copy.wait_recv()
    sums = small_conv(laterals, small_h, mm, lambda t: t)
    grads = []
    for i, (cot, level_out) in enumerate(((cot16, lev16), (cotc, levc))):
        unit, scale = normed(sums[i])
        gain = gains[2 + i, 1:2]
        level_out[...] = (unit * gain + offsets[2 + i, 1:2]).astype(BF16).reshape(level_out.shape)
        grads.append(norm_back(unit, scale, cot[...].reshape(-1, 256).astype(F32) * gain).astype(BF16))
    grads = jnp.concatenate(grads)
    back_copies = exchange(grads, back_s, back_h)

    z_ring = [(z - turn + 4) % 4, (z + turn + 4) % 4, (z + 2) % 4]
    y_ring = [4 + (y - turn + 4) % 4, 4 + (y + turn + 4) % 4, 4 + (y + 2) % 4]
    (z_on,) = pass_on(z_up, z_ring[0], [z_ahead])
    (y_on,) = pass_on(y_up, y_ring[0], [y_ahead])
    pass_on(z_down, z_ring[1], [])
    pass_on(y_down, y_ring[1], [])

    for copy in a_copies:
        copy.wait_recv()
    tile = at[...].reshape(OWN, 1280)
    row = lax.broadcasted_iota(jnp.int32, (1280, 256), 0)
    column = lax.broadcasted_iota(jnp.int32, (1280, 256), 1)
    row = jnp.where(column % 16 < 10, row - column // 16 * 80 - column % 16, -1)

    @pl.loop(0, 8)
    def attn_columns(j):
        attn_c[j] = mm(tile, (row == 10 * j).astype(F32).astype(BF16)).astype(BF16)

    attn_copies = [
        copies.start(attn_c.at[(tc + o) % 8], attn_h.at[tc], along[o - 1]) for o in range(1, 8)
    ]
    attn_h[tc] = attn_c[tc]

    for copy in back_copies:
        copy.wait_recv()
    sums = small_conv(grads, back_h, mt, lambda t: 8 - t)
    steps = []
    for i, weight in enumerate((l16, lc)):
        unit, scale = units[i]
        steps.append(mt(norm_back(unit, scale, sums[i] * gains[2 + i, 0:1]).astype(BF16), weight[...]))
    hits = [jnp.where(q.astype(F32) == coarse.astype(F32), 1.0, 0.0) for q in quads]
    portion = steps[1] / (hits[0] + hits[1] + hits[2] + hits[3])
    total = steps[0]
    for q in range(4):
        total = total + mm(quad_t[q], (hits[q] * portion).astype(BF16))
    dx_small[...] = total

    for copy in halo_copies + cot_copies:
        copy.wait_recv()
    xe[:OWN] = x
    xe[OWN:] = pick(ring_sel[...], xh[...].reshape(128, 1280))
    ring4[...] = pick(cot_ring4[...], cot_h[...]).reshape(4, 4, RING, 256)
    ring8[...] = pick(cot_ring8[...], cot_h[...]).reshape(2, 2, RING, 256)
    pass_on(z_on, z_ring[2], [])
    pass_on(y_on, y_ring[2], [])
    for copy in shared:
        copy.wait_recv()
    keep = exists_mask(TOK, RING_SPANS)
    bias1, gain_m, shift_m = (ref[...].reshape(1, 640) for ref in (bias1, gain_m, shift_m))
    for p in range(4):
        cols = pl.ds(640 * p, 640)
        pre = mm(xe[...], w[:, cols]) + bias1
        unit, size = normed(pre)
        before = unit * gain_m + shift_m
        cdf = 0.5 * (1 + erf(before * (0.5**0.5)))
        up[p] = (before * cdf).astype(BF16)
        inner = before[:OWN]
        unit_u[p] = unit[:OWN]
        scale_u[p] = size[:OWN]
        slope_u[p] = (cdf[:OWN] + inner * jnp.exp(-0.5 * inner * inner) * (1 / np.sqrt(2 * np.pi))) * gain_m
    for p in range(4):
        for q in range(4):
            ph, pw = 2 * (p // 2) + q // 2, 2 * (p % 2) + q % 2
            pre = mt(up[p], c2t[q]) + bias4
            unit, size = normed(pre)
            unit_l[ph, pw] = unit[:OWN]
            scale_l[ph, pw] = size[:OWN]
            lat[ph + 1, pw + 1] = ((unit * gains[0, 0:1] + offsets[0, 0:1]) * keep).astype(BF16)
    def done4(ph, pw, grads):
        d4[2 * (ph // 2) + pw // 2, 2 * (ph % 2) + pw % 2] = grads

    def done8(ph, pw, grads):
        d8[2 * ph + pw] = grads

    d8 = d4.at[4]
    pyramid_level(
        4, lat, back, unit_l, scale_l, conv.at[0], cot4, ring4, out4, gains[0], offsets[0], keep, shifts, split4, done4
    )
    for p in range(4):
        cols = pl.ds(2560 + 256 * p, 256)
        pre = mm(xe[...], w[:, cols]) + bias8
        unit, size = normed(pre)
        unit_l[p // 2, p % 2] = unit[:OWN]
        scale_l[p // 2, p % 2] = size[:OWN]
        lat[p // 2 + 1, p % 2 + 1] = ((unit * gains[1, 0:1] + offsets[1, 0:1]) * keep).astype(BF16)

    pyramid_level(
        2, lat, back, unit_l, scale_l, conv.at[1], cot8, ring8, out8, gains[1], offsets[1], keep, shifts, split8, done8
    )
    dup = jnp.zeros((4 * OWN, 640), F32)
    for q in range(4):
        block = jnp.concatenate([d4[p, q] for p in range(4)], axis=0)
        dup = dup + mm(block, c2t[q])
    for p in range(4):
        grads = norm_back(unit_u[p], scale_u[p], dup[p * OWN : p * OWN + OWN] * slope_u[p])
        dfull[:, 640 * p : 640 * p + 640] = grads.astype(BF16)
        dfull[:, 2560 + 256 * p : 2816 + 256 * p] = d4[4, p]
    block_at = [tc, (tc - 2 * turn + 8) % 8, (tc + 2 * turn + 8) % 8, (tc + 4) % 8]
    twins = [[], []]

    def forward_tile(h, slot, peers):
        block = tiles.at[h, slot]
        twins[h].append(copies.start(block, block, sibling))
        return [copies.start(block, block, peer) for peer in peers]

    rings, homes = [], []
    for h in range(2):
        cols = pl.ds(640 * h, 640)
        grads = (mt(dfull[...], w[cols]) + dx_small[:, cols]).astype(BF16).reshape(8, 16, 640)
        mine[h] = grads
        block = tiles.at[h, tc]
        rings.append([copies.start(mine.at[h], block, peer) for peer in (z_ahead, z_behind)])
        twins[h].append(copies.start(mine.at[h], block, sibling))
        homes += [copies.start(mine.at[h, (tc + o) % 8], home.at[h, tc], across[o]) for o in range(8)]
        tiles[h, tc] = grads
    for copy in attn_copies:
        copy.wait_recv()
    for j in range(8):
        attn_t[:, 128 * j : 128 * j + 128] = attn_h[j].T
    onward = []
    for h in range(2):
        rings[h][0].wait_recv()
        onward += forward_tile(h, block_at[1], [z_ahead])
    sums = []
    for h in range(2):
        rings[h][1].wait_recv()
        forward_tile(h, block_at[2], [])
        onward[h].wait_recv()
        forward_tile(h, block_at[3], [])
        for copy in twins[h]:
            copy.wait_recv()
        product = mm(attn_t[...], tiles[h].reshape(8 * OWN, 640))
        part[h] = product.astype(BF16).reshape(16, 16, 640)
        sums += [
            copies.start(part.at[h, (me + o) % 16], parts.at[h, me], plane[o - 1]) for o in range(1, 16)
        ]
        parts[h, me] = part[h, me]
    for copy in homes:
        copy.wait_recv()
    home_out[...] = home[...]
    for copy in sums:
        copy.wait_recv()
    parts_out[...] = parts[...]
    copies.finish()


def shape(dims, dtype=BF16):
    return jax.ShapeDtypeStruct(dims, dtype)


def call(kernel, outs, scratch, args, collective_id=None, specs=None):
    vmem = pl.BlockSpec(memory_space=pltpu.VMEM)
    params = {"vmem_limit_bytes": 62 * 2**20}
    if collective_id is not None:
        params.update(collective_id=collective_id, has_side_effects=True)
    return pl.pallas_call(
        kernel,
        out_shape=outs,
        in_specs=specs or [vmem] * len(args),
        out_specs=[vmem] * len(outs),
        scratch_shapes=scratch,
        compiler_params=pltpu.CompilerParams(**params),
    )(*args)


def buffer(*dims):
    return pltpu.VMEM(dims, BF16)


def erf(x):
    x = jnp.clip(x, -3.832506856900711, 3.832506856900711)
    square = x * x
    over = jnp.full_like(x, 0.00022905065861350646)
    for c in (0.0034082910107109506, 0.050955695062380861, 0.18520832239976145, 1.128379143519084):
        over = over * square + c
    under = jnp.full_like(x, -1.1791602954361697e-7)
    for c in (0.000023547966471313185, 0.0010179625278914885, 0.014070470171167667,
              0.11098505178285362, 0.49746925110067538, 1.0):
        under = under * square + c
    return x * over / under


def fill_shifted(padded, n, shifts):
    for i in range(n + 2):
        for j in range(n + 2):
            dy, dx = (i - 1) // n, (j - 1) // n
            if dy or dx:
                source = padded[(i - 1) % n + 1, (j - 1) % n + 1]
                padded[i, j] = mm(shifts[3 * dy + dx + 4], source).astype(BF16)


def pyramid_level(n, lat, back, unit, scale, conv, cot, ring, out, gains, offsets, keep, shifts, split, done):
    groups = n * n // 8 if n == 4 else 1
    rows = ROWS // groups
    fill_shifted(lat, n, shifts)

    @pl.loop(0, n)
    def forward(ph):
        acc = jnp.zeros((n * TOK, 256), F32)
        for t in range(9):
            dy, dx = t // 3, t % 3
            block = lat[ph + dy, dx : dx + n].reshape(n * TOK, 256)
            acc = acc + mm(block, conv[t])
        pieces = []
        for g in range(groups):
            block = cot[pl.ds(rows * g, rows), ph].reshape(256, 256)
            pieces.append(mm(split[1], block))
        tokens = 256 // n
        results = []
        for pw in range(n):
            values, size = normed(acc[pw * TOK : pw * TOK + TOK])
            results.append((values[:OWN] * gains[1:2] + offsets[1:2]).astype(BF16))
            own = [piece[pw * tokens : pw * tokens + tokens] for piece in pieces]
            grads = jnp.concatenate(own + [ring[ph, pw].astype(F32)], axis=0)
            grads = norm_back(values, size, grads * gains[1:2])
            back[ph + 1, pw + 1] = (grads * keep).astype(BF16)
        for g in range(groups):
            block = jnp.concatenate([r[g * tokens : g * tokens + tokens] for r in results], axis=0)
            block = mm(split[0], block).astype(BF16)
            out[pl.ds(rows * g, rows), ph] = block.reshape(rows, 8 * n, 256)

    fill_shifted(back, n, shifts)

    @pl.loop(0, n)
    def backward(ph):
        acc = jnp.zeros((n * OWN, 256), F32)
        for t in range(9):
            dy, dx = t // 3, t % 3
            block = jnp.concatenate([back[ph + dy, dx + pw, :OWN] for pw in range(n)], axis=0)
            acc = acc + mt(block, conv[8 - t])
        for pw in range(n):
            grads = acc[pw * OWN : pw * OWN + OWN] * gains[0:1]
            done(ph, pw, norm_back(unit[ph, pw], scale[ph, pw], grads).astype(BF16))


def main(*args):
    def wide(*dims):
        return pltpu.VMEM(dims, F32)

    vmem, anywhere = pl.BlockSpec(memory_space=pltpu.VMEM), pl.BlockSpec(memory_space=pl.ANY)
    specs = [anywhere if i in (2, 3) else vmem for i in range(len(args))]
    copies = 8 + 4 + 8 + 8 + 8 + 8 + 8 + 8 + 4 + 16 + 3 + 7 + 2 * (2 + 1 + 8 + 1 + 3 + 15)
    return call(
        main_kernel,
        [
            shape((16, 4, 32, 256)), shape((16, 2, 16, 256)), shape((16, 8, 256)), shape((8, 4, 256)),
            shape((2, 8, 16, 640)), shape((2, 16, 16, 640)),
        ],
        [
            buffer(1280, 3584), buffer(5, 80, 2, 2, 640), buffer(5, 80, 2, 2, 640),
            buffer(8, 16, 1280), buffer(8, 16, 1280), buffer(8, 16, 1280), buffer(8, 16, 1280),
            buffer(8, 16, 1280), buffer(2, 16, 1280),
            buffer(SMALL, 256), buffer(SMALL, 256), buffer(SMALL, 256), buffer(SMALL, 256),
            buffer(COT, 256), buffer(COT, 256), buffer(8, OWN, 256), buffer(8, OWN, 256),
            buffer(TOK, 1280), buffer(4, 256, 640), buffer(4, 4, RING, 256), buffer(2, 2, RING, 256),
            wide(OWN, 1280), buffer(4, TOK, 640), wide(4, OWN, 640), wide(4, OWN, 640), wide(4, OWN, 1),
            buffer(6, 6, TOK, 256), buffer(6, 6, TOK, 256), wide(4, 4, OWN, 256), wide(4, 4, OWN, 1),
            buffer(5, 4, OWN, 256), buffer(OWN, 3584), buffer(256, 1024),
            buffer(2, 8, 16, 640), buffer(2, 8, 16, 640), buffer(2, 8, 8, 16, 640),
            buffer(2, 16, 16, 640), buffer(2, 16, 16, 640),
            pltpu.SemaphoreType.DMA((copies,)), pltpu.SemaphoreType.DMA((copies,)),
            pltpu.SemaphoreType.DMA((2, 5)),
        ],
        args,
        collective_id=0,
        specs=specs,
    )


def finish_kernel(home, parts, *levels_and_outs):
    ins, (grads, weight), outs = levels_and_outs[:4], levels_and_outs[4:6], levels_and_outs[6:]
    for h in range(2):
        cols = slice(640 * h, 640 * h + 640)
        for j in range(8):
            for i in range(2):
                grads[64 * i + 8 * j : 64 * i + 8 * j + 8, cols] = home[h, j, 8 * i : 8 * i + 8]
        total = parts[h, 0].astype(F32)
        for j in range(1, 16):
            total = total + parts[h, j].astype(F32)
        weight[:, cols] = total[:10]
    for level_in, level_out in zip(ins, outs):
        level_out[...] = level_in[...]


def finish(home, parts, *levels):
    return call(
        finish_kernel,
        [shape((OWN, 1280)), shape((10, 1280), F32)] + [shape(level.shape) for level in levels],
        [],
        (home, parts) + levels,
    )


def body(
    features,
    attn_hidden,
    first_deconv,
    first_bias,
    mid_gain,
    mid_shift,
    second_deconv,
    second_bias,
    half_deconv,
    half_bias,
    lateral_four,
    lateral_eight,
    lateral_sixteen,
    lateral_coarse,
    output_conv,
    level_gain,
    level_shift,
    cotangent_four,
    cotangent_eight,
    cotangent_sixteen,
    cotangent_coarse,
):
    k2t = second_deconv.transpose(1, 2, 3, 0).reshape(4, 320, 640)
    conv = output_conv.reshape(4, 9, 256, 256)
    cot4 = cotangent_four.reshape(16, 4, 32, 256)
    cot8 = cotangent_eight.reshape(16, 2, 16, 256)
    quads = quad_pick()
    rings = cot_ring(4), cot_ring(2)
    split4, split8 = (const(np.stack([interleave(n), interleave(n).T])) for n in (4, 2))
    out4, out8, lev16, levc, home, parts = main(
        features[0], attn_hidden[0], first_deconv, half_deconv, k2t,
        lateral_four, lateral_eight, lateral_sixteen, lateral_coarse, second_bias, half_bias,
        conv, level_gain, level_shift, cot4, cot8, cotangent_sixteen[0], cotangent_coarse[0],
        const(chunk_split()), const(column_pick()), const(ring_pick()), const(small_send()),
        const(small_taps()), const(quads), const(quads.transpose(0, 2, 1)), const(cot_pick()),
        const(rings[0]), const(rings[1]),
        const(shift_matrices().reshape(9, TOK, TOK)), split4, split8,
        first_bias, mid_gain, mid_shift,
    )
    grads, weight, out4, out8, lev16, levc = finish(home, parts, out4, out8, lev16, levc)
    return (
        out4.reshape(1, 64, 32, 256),
        out8.reshape(1, 32, 16, 256),
        lev16[None],
        levc[None],
        grads[None],
        weight,
    )


def solution(mesh):
    tokens = P("segment", ("tr", "tc"), None)
    deconv = P("segment", None, None, None)
    grid = P("segment", "tr", "tc", None)
    placed = (
        (tokens, tokens, deconv) + (P(),) * 5 + (deconv,) + (P(),) * 8 + (grid,) * 4
    )
    return jax.shard_map(
        body,
        mesh=mesh,
        in_specs=placed,
        out_specs=(grid, grid, grid, grid, tokens, P(("segment", "tr", "tc"), None)),
        check_vma=False,
    )
```

```python
import jax
import jax.numpy as jnp
import numpy as np
from jax import lax
from jax.experimental import pallas as pl
from jax.experimental.pallas import tpu as pltpu
from jax.sharding import PartitionSpec as P

EPS = 1e-06
F32 = jnp.float32
BF16 = jnp.bfloat16
MESH = pl.DeviceIdType.MESH

ROWS, COLS = 16, 8
OWN, RING = 128, 64
TOK = OWN + RING
DIRS = ((-1, 0), (1, 0), (0, -1), (0, 1), (-1, -1), (-1, 1), (1, -1), (1, 1))
OPPOSITE = (1, 0, 3, 2, 7, 6, 5, 4)


def token_index(r, c):
    if not (-1 <= r <= ROWS and -1 <= c <= COLS):
        return None
    if 0 <= r < ROWS and 0 <= c < COLS:
        return r * COLS + c
    if 0 <= c < COLS:
        return OWN + (0 if r < 0 else 8) + c
    if 0 <= r < ROWS:
        return OWN + (16 if c < 0 else 32) + r
    return OWN + 48 + (0 if r < 0 else 2) + (0 if c < 0 else 1)


TOKENS_AT = [(r, c) for r in range(-1, ROWS + 1) for c in range(-1, COLS + 1)]


def shift_matrices():
    out = np.zeros((3, 3, TOK, TOK), np.float32)
    for r, c in TOKENS_AT:
        for dy in range(-1, 2):
            for dx in range(-1, 2):
                there = token_index(r + dy, c + dx)
                if there is not None:
                    out[dy + 1, dx + 1, token_index(r, c), there] = 1
    return out


def ring_pick():
    out = np.zeros((RING, 128), np.float32)
    for c in range(8):
        out[c, 0 * 16 + 8 + c] = 1
        out[8 + c, 1 * 16 + c] = 1
    for r in range(16):
        out[16 + r, 2 * 16 + r] = 1
        out[32 + r, 3 * 16 + r] = 1
    out[48, 4 * 16 + 15] = 1
    out[49, 5 * 16 + 8] = 1
    out[50, 6 * 16 + 7] = 1
    out[51, 7 * 16 + 0] = 1
    return out


def column_pick():
    out = np.zeros((32, 128), np.float32)
    for r in range(16):
        out[r, r * 8] = 1
        out[16 + r, r * 8 + 7] = 1
    return out


SMALL_SIZE = (16, 16, 32, 32, 16, 16, 16, 16)
SMALL_AT = tuple(int(v) for v in np.cumsum((0,) + SMALL_SIZE)[:8])
SMALL = sum(SMALL_SIZE)


def edge_pixels(height, width, k):
    dy, dx = DIRS[k]
    rows = range(height) if dy == 0 else ([0] if dy < 0 else [height - 1])
    cols = range(width) if dx == 0 else ([0] if dx < 0 else [width - 1])
    return [(r, c) for r in rows for c in cols]


def small_send():
    out = np.zeros((SMALL, 160), np.float32)
    for k in range(8):
        at = SMALL_AT[k]
        for r, c in edge_pixels(16, 8, k):
            out[at, r * 8 + c] = 1
            at += 1
        for r, c in edge_pixels(8, 4, k):
            out[at, 128 + r * 4 + c] = 1
            at += 1
    return out


def halo_slot(height, width, r, c):
    k = DIRS.index(((r >= height) - (r < 0), (c >= width) - (c < 0)))
    return k, edge_pixels(height, width, OPPOSITE[k]).index((r % height, c % width))


def small_taps():
    out = np.zeros((9, 160, 160 + SMALL), np.float32)
    for base, height, width in ((0, 16, 8), (128, 8, 4)):
        for t in range(9):
            for r in range(height):
                for c in range(width):
                    rr, cc = r + t // 3 - 1, c + t % 3 - 1
                    if 0 <= rr < height and 0 <= cc < width:
                        out[t, base + r * width + c, base + rr * width + cc] = 1
                    else:
                        k, place = halo_slot(height, width, rr, cc)
                        place += len(edge_pixels(16, 8, OPPOSITE[k])) if base else 0
                        out[t, base + r * width + c, 160 + SMALL_AT[k] + place] = 1
    return out


COT_SIZE = (48, 48, 96, 96, 16, 16, 16, 16)
COT_AT = tuple(int(v) for v in np.cumsum((0,) + COT_SIZE)[:8])
COT = sum(COT_SIZE)


def cot_send():
    index = np.full((COT,), -1)
    for k in range(8):
        at = COT_AT[k]
        for r, c in edge_pixels(64, 32, k):
            index[at] = r * 32 + c
            at += 1
        for r, c in edge_pixels(32, 16, k):
            index[at] = 2048 + r * 16 + c
            at += 1
    return index


def cot_ring(n):
    height, width = ROWS * n, COLS * n
    out = np.zeros((n, n, RING, COT), np.float32)
    for r, c in TOKENS_AT:
        if 0 <= r < ROWS and 0 <= c < COLS:
            continue
        for ph in range(n):
            for pw in range(n):
                y, x = r * n + ph, c * n + pw
                if -1 <= y <= height and -1 <= x <= width:
                    k, place = halo_slot(height, width, y, x)
                    place += len(edge_pixels(64, 32, OPPOSITE[k])) if n == 2 else 0
                    out[ph, pw, token_index(r, c) - OWN, COT_AT[k] + place] = 1
    return out.reshape(n * n * RING, COT)


def interleave(n):
    tokens = 256 // n
    out = np.zeros((256, 256), np.float32)
    for t in range(tokens):
        for p in range(n):
            out[t * n + p, p * tokens + t] = 1
    return out


def quad_pick():
    out = np.zeros((4, 32, 128), np.float32)
    for q in range(4):
        for r in range(8):
            for c in range(4):
                out[q, r * 4 + c, (2 * r + q // 2) * 8 + 2 * c + q % 2] = 1
    return out


def chunk_split():
    out = np.zeros((320, 320), np.float32)
    for e in range(80):
        for p in range(4):
            out[p * 80 + e, e * 4 + p] = 1
    return out


def cot_pick():
    index = cot_send()
    out = np.zeros((COT, 2560), np.float32)
    for row, at in enumerate(index):
        if at >= 0:
            out[row, at] = 1
    return out


def const(array):
    return jnp.asarray(array, BF16)


def mm(a, b):
    return jnp.dot(a, b, preferred_element_type=F32)


def mt(a, b):
    return lax.dot_general(a, b, (((1,), (1,)), ((), ())), preferred_element_type=F32)


def pick(selection, a):
    return mm(selection, a).astype(BF16)


def normed(values):
    centre = jnp.mean(values, axis=-1, keepdims=True)
    values = values - centre
    scale = lax.rsqrt(jnp.mean(values * values, axis=-1, keepdims=True) + EPS)
    return values * scale, scale


def norm_back(unit, scale, grad):
    return scale * (
        grad
        - jnp.mean(grad, axis=-1, keepdims=True)
        - unit * jnp.mean(grad * unit, axis=-1, keepdims=True)
    )


def place():
    return lax.axis_index("segment"), lax.axis_index("tr"), lax.axis_index("tc")


def neighbour(k, s, tr, tc):
    dy, dx = DIRS[k]
    return (s, (tr + dy + 8) % 8, (tc + dx + 8) % 8)


def exists_mask(rows, spans):
    _, tr, tc = place()
    row = lax.broadcasted_iota(jnp.int32, (rows, 1), 0)
    mask = jnp.ones((rows, 1), F32)
    for k, lo, hi in spans:
        if k is None:
            there = 0.0
        else:
            dy, dx = DIRS[k]
            inside = (tr + dy >= 0) & (tr + dy < 8) & (tc + dx >= 0) & (tc + dx < 8)
            there = jnp.where(inside, 1.0, 0.0)
        mask = jnp.where((row >= lo) & (row < hi), there, mask)
    return mask


RING_SPANS = (
    (0, 128, 136), (1, 136, 144), (2, 144, 160), (3, 160, 176),
    (4, 176, 177), (5, 177, 178), (6, 178, 179), (7, 179, 180), (None, 180, 192),
)
SMALL_SPANS = tuple((k, SMALL_AT[k], SMALL_AT[k] + SMALL_SIZE[k]) for k in range(8))


def signal_all(peers):
    barrier = pltpu.get_barrier_semaphore()
    for peer in peers:
        pl.semaphore_signal(barrier, inc=1, device_id=peer, device_id_type=MESH)


def wait_all(peers):
    pl.semaphore_wait(pltpu.get_barrier_semaphore(), len(peers))


class Copies:
    def __init__(self, send, recv):
        self.send, self.recv, self.used, self.unsent = send, recv, 0, []

    def start(self, src, dst, peer):
        k, self.used = self.used, self.used + 1
        copy = pltpu.make_async_remote_copy(
            src_ref=src,
            dst_ref=dst,
            send_sem=self.send.at[k],
            recv_sem=self.recv.at[k],
            device_id=peer,
            device_id_type=MESH,
        )
        copy.start()
        self.unsent.append(copy)
        return copy

    def finish(self):
        for copy in self.unsent:
            copy.wait_send()


def split_product(row, weight):
    total = 0.0
    for _ in range(3):
        piece = row.astype(BF16)
        total = total + mm(piece, weight)
        row = row - piece.astype(F32)
    return total


def main_kernel(
    feat, attn, first, half, k2t, l4, l8, l16, lc, b2, bh, conv, gains, offsets, cot4, cot8, cot16, cotc,
    split, columns, ring_sel, edges, taps, quad, quad_t, cot_sel, cot_ring4, cot_ring8,
    shifts, split4, split8, bias1, gain_m, shift_m,
    out4, out8, lev16, levc, home_out, parts_out,
    w, first_v, half_v, xa, aa, xt, xh, sides, small, small_h, back_s, back_h, cotm, cot_h, attn_c, attn_h,
    xe, c2t, ring4, ring8, dx_small, up, unit_u, slope_u, scale_u, lat, back, unit_l, scale_l, d4, dfull,
    res4, res8, attn_t, mine, home, tiles, part, parts, send, recv, load,
):
    s, tr, tc = place()
    other = 1 - s
    x_hi, y, z, core = tr // 4, tr % 4, tc // 2, tc % 2
    turn = 1 - 2 * core
    far = (other, (1 - x_hi) * 4 + y, tc)
    balance = (other, (1 - x_hi + core * (2 * x_hi - 1)) * 4 + y, tc)
    sibling = (s, tr, tc + turn)
    z_ahead = (s, tr, (z + turn + 4) % 4 * 2 + core)
    z_behind = (s, tr, (z - turn + 4) % 4 * 2 + core)
    y_ahead = (s, x_hi * 4 + (y + turn + 4) % 4, tc)
    y_behind = (s, x_hi * 4 + (y - turn + 4) % 4, tc)
    around = [neighbour(k, s, tr, tc) for k in range(8)]
    across = [(other, tr, (tc + o) % 8) for o in range(8)]
    me = s * 8 + tr
    plane = [((me + o) % 16 // 8, (me + o) % 8, tc) for o in range(1, 16)]
    peers = plane + across[1:] + around[2:] + [z_ahead, z_behind]
    signal_all(peers)
    copies = Copies(send, recv)

    def chunk_at(i):
        return i % 2 * 4 + (jnp.where(i % 2 == 0, z, y) + i // 2) % 4

    def loads(slot):
        rows = pl.ds(chunk_at(order[slot]) * 80, 80)
        return [
            pltpu.make_async_copy(ref.at[rows], slots.at[slot % 4], load.at[k, slot % 4])
            for k, (ref, slots) in enumerate(((first, first_v), (half, half_v)))
        ]

    def relayout(slot):
        for copy in loads(slot):
            copy.wait()
        block = mm(split[...], first_v[slot % 4].reshape(320, 640)).astype(BF16)
        product = mm(half_v[slot % 4].reshape(320, 640), l8[...]).astype(BF16)
        product = mm(split[...], product).astype(BF16)
        rows = pl.ds(pl.multiple_of(640 * s + chunk_at(order[slot]) * 80, 16), 80)
        for p in range(4):
            w[rows, 640 * p : 640 * p + 640] = block[80 * p : 80 * p + 80]
            w[rows, 2560 + 256 * p : 2816 + 256 * p] = product[80 * p : 80 * p + 80]
        return w.at[rows]

    order = [0, 1, 2 + core, 4 + core, 6 + core]

    def piece(owner, chunk, h):
        rows = pl.ds(pl.multiple_of(640 * owner + chunk * 80, 16), 80)
        start, width = ((2560 + 512 * core, 512), (1280 * core, 1280))[h]
        return w.at[rows, pl.ds(pl.multiple_of(start, 128), width)]

    shared = [[], []]

    def send_piece(h, chunk, peer, owner):
        part = piece(owner, chunk, h)
        return copies.start(part, part, peer)

    def pass_on(h, arrived, chunk, peers):
        arrived.wait_recv()
        sent = [send_piece(h, chunk, peer, other) for peer in peers]
        shared[h].append(send_piece(h, chunk, sibling, other))
        return sent

    z_ring = [(z - turn + 4) % 4, (z + turn + 4) % 4, (z + 2) % 4]
    y_ring = [4 + (y - turn + 4) % 4, 4 + (y + turn + 4) % 4, 4 + (y + 2) % 4]
    z_hops, y_hops = [None, None], [None, None]

    def first_hop_z(h):
        z_hops[h] = pass_on(h, z_first[h], z, [z_ahead, z_behind])

    def first_hop_y(h):
        y_hops[h] = pass_on(h, y_first[h], 4 + y, [y_ahead, y_behind])

    def second_hop(h):
        for hops, ring, ahead in ((z_hops, z_ring, z_ahead), (y_hops, y_ring, y_ahead)):
            up, down = hops[h]
            hops[h] = pass_on(h, up, ring[0], [ahead])
            pass_on(h, down, ring[1], [])

    def third_hop(h):
        for hops, ring in ((z_hops, z_ring), (y_hops, y_ring)):
            pass_on(h, hops[h][0], ring[2], [])

    for slot in range(4):
        for copy in loads(slot):
            copy.start()
    for j in range(8):
        for i in range(2):
            xa[j, 8 * i : 8 * i + 8] = feat[64 * i + 8 * j : 64 * i + 8 * j + 8]
            aa[j, 8 * i : 8 * i + 8] = attn[64 * i + 8 * j : 64 * i + 8 * j + 8]
    relayout(0)
    for copy in loads(4):
        copy.start()
    wait_all(peers)
    z_first = [send_piece(0, z, far, s)]
    x_copies = [copies.start(xa.at[(tc + o) % 8], xt.at[tc], across[o]) for o in range(8)]
    z_first.append(send_piece(1, z, far, s))
    relayout(1)
    y_first = [send_piece(h, 4 + y, balance, s) for h in range(2)]
    pixels = jnp.concatenate([cot4[...].reshape(2048, 256), cot8[...].reshape(512, 256)])
    cotm[...] = pick(cot_sel[...], pixels)
    cot_copies = [
        copies.start(
            cotm.at[pl.ds(COT_AT[k], COT_SIZE[k])],
            cot_h.at[pl.ds(COT_AT[OPPOSITE[k]], COT_SIZE[k])],
            around[k],
        )
        for k in range(8)
    ]
    for slot in range(2, 5):
        rows = relayout(slot)
        shared[0].append(copies.start(rows, rows, sibling))
    first_hop_z(0)
    first_hop_y(0)
    tile = aa[...].reshape(OWN, 1280)
    row = lax.broadcasted_iota(jnp.int32, (1280, 256), 0)
    column = lax.broadcasted_iota(jnp.int32, (1280, 256), 1)
    row = jnp.where(column % 16 < 10, row - column // 16 * 80 - column % 16, -1)

    @pl.loop(0, 8)
    def attn_columns(j):
        attn_c[j] = mm(tile, (row == 10 * j).astype(F32).astype(BF16)).astype(BF16).reshape(8, 16, 256)

    for p in range(4):
        c2t[p] = lax.dot_general(
            l4[...], k2t[p], (((0,), (0,)), ((), ())), preferred_element_type=F32
        ).astype(BF16)
    bias4 = split_product(b2[...].reshape(1, 320), l4[...])
    bias8 = split_product(bh[...].reshape(1, 640), l8[...])
    for copy in cot_copies:
        copy.wait_recv()
    ring4[...] = pick(cot_ring4[...], cot_h[...]).reshape(4, 4, RING, 256)
    ring8[...] = pick(cot_ring8[...], cot_h[...]).reshape(2, 2, RING, 256)
    second_hop(0)
    first_hop_z(1)

    for copy in x_copies:
        copy.wait_recv()
    x = xt[...].reshape(OWN, 1280)
    sides[...] = pick(columns[...], x).reshape(2, 16, 1280)
    sources = (xt.at[0], xt.at[7], sides.at[0], sides.at[1], xt.at[0], xt.at[0], xt.at[7], xt.at[7])
    halo_copies = [copies.start(sources[k], xh.at[OPPOSITE[k]], around[k]) for k in range(8)]
    quads = [pick(quad[q], x) for q in range(4)]
    coarse = jnp.maximum(jnp.maximum(quads[0], quads[1]), jnp.maximum(quads[2], quads[3]))
    units = [normed(mm(x, l16[...])), normed(mm(coarse, lc[...]))]
    laterals = jnp.concatenate(
        [(units[i][0] * gains[2 + i, 0:1] + offsets[2 + i, 0:1]).astype(BF16) for i in range(2)]
    )

    def exchange(rows, message, halo):
        message[...] = pick(edges[...], rows)
        return [
            copies.start(
                message.at[pl.ds(SMALL_AT[k], SMALL_SIZE[k])],
                halo.at[pl.ds(SMALL_AT[OPPOSITE[k]], SMALL_SIZE[k])],
                around[k],
            )
            for k in range(8)
        ]

    def small_conv(rows, halo, product, order):
        both = jnp.concatenate([rows, (halo[...] * exists_mask(SMALL, SMALL_SPANS)).astype(BF16)])
        sums = [jnp.zeros((128, 256), F32), jnp.zeros((32, 256), F32)]
        for t in range(9):
            moved = pick(taps[t], both)
            for i, (lo, hi) in enumerate(((0, 128), (128, 160))):
                sums[i] = sums[i] + product(moved[lo:hi], conv[2 + i, order(t)])
        return sums

    small_copies = exchange(laterals, small, small_h)
    first_hop_y(1)
    third_hop(0)
    for copy in halo_copies:
        copy.wait_recv()
    xe[:OWN] = x
    xe[OWN:] = pick(ring_sel[...], xh[...].reshape(128, 1280))
    for copy in shared[0]:
        copy.wait_recv()
    keep = exists_mask(TOK, RING_SPANS)

    def done8(ph, pw, grads):
        d8[2 * ph + pw] = grads

    d8 = d4.at[4]
    for p in range(4):
        cols = pl.ds(2560 + 256 * p, 256)
        pre = mm(xe[...], w[:, cols]) + bias8
        unit, size = normed(pre)
        unit_l[p // 2, p % 2] = unit[:OWN]
        scale_l[p // 2, p % 2] = size[:OWN]
        lat[p // 2 + 1, p % 2 + 1] = ((unit * gains[1, 0:1] + offsets[1, 0:1]) * keep).astype(BF16)

    pyramid_level(
        2, lat, back, unit_l, scale_l, conv.at[1], cot8, ring8, res8, gains[1], offsets[1], keep, shifts, split8, done8,
        lambda: second_hop(1),
    )

    for copy in small_copies:
        copy.wait_recv()
    sums = small_conv(laterals, small_h, mm, lambda t: t)
    grads = []
    for i, (cot, level_out) in enumerate(((cot16, lev16), (cotc, levc))):
        unit, scale = normed(sums[i])
        gain = gains[2 + i, 1:2]
        level_out[...] = (unit * gain + offsets[2 + i, 1:2]).astype(BF16).reshape(level_out.shape)
        grads.append(norm_back(unit, scale, cot[...].reshape(-1, 256).astype(F32) * gain).astype(BF16))
    grads = jnp.concatenate(grads)
    back_copies = exchange(grads, back_s, back_h)

    third_hop(1)
    for copy in shared[1]:
        copy.wait_recv()
    attn_copies = [
        copies.start(attn_c.at[(tc + o) % 8], attn_h.at[pl.ds(0, 8), tc], across[o]) for o in range(8)
    ]

    bias1, gain_m, shift_m = (ref[...].reshape(1, 640) for ref in (bias1, gain_m, shift_m))
    for p in range(4):
        cols = pl.ds(640 * p, 640)
        pre = mm(xe[...], w[:, cols]) + bias1
        unit, size = normed(pre)
        before = unit * gain_m + shift_m
        cdf = 0.5 * (1 + erf(before * (0.5**0.5)))
        up[p] = (before * cdf).astype(BF16)
        inner = before[:OWN]
        unit_u[p] = unit[:OWN]
        scale_u[p] = size[:OWN]
        slope_u[p] = (cdf[:OWN] + inner * jnp.exp(-0.5 * inner * inner) * (1 / np.sqrt(2 * np.pi))) * gain_m
    for copy in back_copies:
        copy.wait_recv()
    sums = small_conv(grads, back_h, mt, lambda t: 8 - t)
    steps = []
    for i, weight in enumerate((l16, lc)):
        unit, scale = units[i]
        steps.append(mt(norm_back(unit, scale, sums[i] * gains[2 + i, 0:1]).astype(BF16), weight[...]))
    hits = [jnp.where(q.astype(F32) == coarse.astype(F32), 1.0, 0.0) for q in quads]
    portion = steps[1] / (hits[0] + hits[1] + hits[2] + hits[3])
    total = steps[0]
    for q in range(4):
        total = total + mm(quad_t[q], (hits[q] * portion).astype(BF16))
    dx_small[...] = total

    for p in range(4):
        for q in range(4):
            ph, pw = 2 * (p // 2) + q // 2, 2 * (p % 2) + q % 2
            pre = mt(up[p], c2t[q]) + bias4
            unit, size = normed(pre)
            unit_l[ph, pw] = unit[:OWN]
            scale_l[ph, pw] = size[:OWN]
            lat[ph + 1, pw + 1] = ((unit * gains[0, 0:1] + offsets[0, 0:1]) * keep).astype(BF16)
    def done4(ph, pw, grads):
        d4[2 * (ph // 2) + pw // 2, 2 * (ph % 2) + pw % 2] = grads

    pyramid_level(
        4, lat, back, unit_l, scale_l, conv.at[0], cot4, ring4, res4, gains[0], offsets[0], keep, shifts, split4, done4
    )
    dup = jnp.zeros((4 * OWN, 640), F32)
    for q in range(4):
        block = jnp.concatenate([d4[p, q] for p in range(4)], axis=0)
        dup = dup + mm(block, c2t[q])
    for p in range(4):
        grads = norm_back(unit_u[p], scale_u[p], dup[p * OWN : p * OWN + OWN] * slope_u[p])
        dfull[:, 640 * p : 640 * p + 640] = grads.astype(BF16)
        dfull[:, 2560 + 256 * p : 2816 + 256 * p] = d4[4, p]
    block_at = [tc, (tc - 2 * turn + 8) % 8, (tc + 2 * turn + 8) % 8, (tc + 4) % 8]
    twins = [[], []]

    def forward_tile(h, slot, peers):
        block = tiles.at[h, slot]
        twins[h].append(copies.start(block, block, sibling))
        return [copies.start(block, block, peer) for peer in peers]

    rings = []
    for h in range(2):
        cols = pl.ds(640 * h, 640)
        grads = (mt(dfull[...], w[cols]) + dx_small[:, cols]).astype(BF16).reshape(8, 16, 640)
        mine[h] = grads
        block = tiles.at[h, tc]
        rings.append([copies.start(mine.at[h], block, peer) for peer in (z_ahead, z_behind)])
        twins[h].append(copies.start(mine.at[h], block, sibling))
        tiles[h, tc] = grads
    homes = [
        copies.start(mine.at[h, (tc + o) % 8], home.at[h, tc], across[o]) for h in range(2) for o in range(8)
    ]
    for copy in attn_copies:
        copy.wait_recv()
    for j in range(8):
        attn_t[:, 128 * j : 128 * j + 128] = attn_h[j].reshape(OWN, 256).T
    onward = []
    for h in range(2):
        rings[h][0].wait_recv()
        onward += forward_tile(h, block_at[1], [z_ahead])
    join_level(4, res4, out4, split4)
    join_level(2, res8, out8, split8)
    sums = []
    for h in range(2):
        rings[h][1].wait_recv()
        forward_tile(h, block_at[2], [])
        onward[h].wait_recv()
        forward_tile(h, block_at[3], [])
        for copy in twins[h]:
            copy.wait_recv()
        product = mm(attn_t[...], tiles[h].reshape(8 * OWN, 640))
        part[h] = product.astype(BF16).reshape(16, 16, 640)
        sums += [
            copies.start(part.at[h, (me + o) % 16], parts.at[h, me], plane[o - 1]) for o in range(1, 16)
        ]
        parts[h, me] = part[h, me]
    for copy in homes:
        copy.wait_recv()
    home_out[...] = home[...]
    for copy in sums:
        copy.wait_recv()
    parts_out[...] = parts[...]
    copies.finish()


def shape(dims, dtype=BF16):
    return jax.ShapeDtypeStruct(dims, dtype)


def call(kernel, outs, scratch, args, collective_id=None, specs=None):
    vmem = pl.BlockSpec(memory_space=pltpu.VMEM)
    params = {"vmem_limit_bytes": 62 * 2**20}
    if collective_id is not None:
        params.update(collective_id=collective_id, has_side_effects=True)
    return pl.pallas_call(
        kernel,
        out_shape=outs,
        in_specs=specs or [vmem] * len(args),
        out_specs=[vmem] * len(outs),
        scratch_shapes=scratch,
        compiler_params=pltpu.CompilerParams(**params),
    )(*args)


def buffer(*dims):
    return pltpu.VMEM(dims, BF16)


def erf(x):
    x = jnp.clip(x, -3.832506856900711, 3.832506856900711)
    square = x * x
    over = jnp.full_like(x, 0.00022905065861350646)
    for c in (0.0034082910107109506, 0.050955695062380861, 0.18520832239976145, 1.128379143519084):
        over = over * square + c
    under = jnp.full_like(x, -1.1791602954361697e-7)
    for c in (0.000023547966471313185, 0.0010179625278914885, 0.014070470171167667,
              0.11098505178285362, 0.49746925110067538, 1.0):
        under = under * square + c
    return x * over / under


def fill_shifted(padded, n, shifts):
    for i in range(n + 2):
        for j in range(n + 2):
            dy, dx = (i - 1) // n, (j - 1) // n
            if dy or dx:
                source = padded[(i - 1) % n + 1, (j - 1) % n + 1]
                padded[i, j] = mm(shifts[3 * dy + dx + 4], source).astype(BF16)


def join_level(n, res, out, split):
    groups = n * n // 8 if n == 4 else 1
    rows, tokens = ROWS // groups, 256 // n

    @pl.loop(0, n)
    def join(ph):
        for g in range(groups):
            block = jnp.concatenate([res[ph, pw, g * tokens : g * tokens + tokens] for pw in range(n)], axis=0)
            block = mm(split[0], block).astype(BF16)
            out[pl.ds(rows * g, rows), ph] = block.reshape(rows, 8 * n, 256)


def pyramid_level(
    n, lat, back, unit, scale, conv, cot, ring, res, gains, offsets, keep, shifts, split, done, between=None
):
    groups = n * n // 8 if n == 4 else 1
    rows = ROWS // groups
    fill_shifted(lat, n, shifts)

    @pl.loop(0, n, unroll=True)
    def forward(ph):
        acc = jnp.zeros((n * TOK, 256), F32)
        for t in range(9):
            dy, dx = t // 3, t % 3
            block = lat[ph + dy, dx : dx + n].reshape(n * TOK, 256)
            acc = acc + mm(block, conv[t])
        pieces = []
        for g in range(groups):
            block = cot[pl.ds(rows * g, rows), ph].reshape(256, 256)
            pieces.append(mm(split[1], block))
        tokens = 256 // n
        for pw in range(n):
            values, size = normed(acc[pw * TOK : pw * TOK + TOK])
            res[ph, pw] = (values[:OWN] * gains[1:2] + offsets[1:2]).astype(BF16)
            own = [piece[pw * tokens : pw * tokens + tokens] for piece in pieces]
            grads = jnp.concatenate(own + [ring[ph, pw].astype(F32)], axis=0)
            grads = norm_back(values, size, grads * gains[1:2])
            back[ph + 1, pw + 1] = (grads * keep).astype(BF16)

    if between is not None:
        between()
    fill_shifted(back, n, shifts)

    @pl.loop(0, n, unroll=True)
    def backward(ph):
        acc = jnp.zeros((n * OWN, 256), F32)
        for t in range(9):
            dy, dx = t // 3, t % 3
            block = jnp.concatenate([back[ph + dy, dx + pw, :OWN] for pw in range(n)], axis=0)
            acc = acc + mt(block, conv[8 - t])
        for pw in range(n):
            grads = acc[pw * OWN : pw * OWN + OWN] * gains[0:1]
            done(ph, pw, norm_back(unit[ph, pw], scale[ph, pw], grads).astype(BF16))


def main(*args):
    def wide(*dims):
        return pltpu.VMEM(dims, F32)

    vmem, anywhere = pl.BlockSpec(memory_space=pltpu.VMEM), pl.BlockSpec(memory_space=pl.ANY)
    specs = [anywhere if i in (2, 3) else vmem for i in range(len(args))]
    copies = 8 + 4 + 8 + 8 + 8 + 8 + 8 + 8 + 4 + 16 + 3 + 2 * (2 + 1 + 8 + 1 + 3 + 15)
    return call(
        main_kernel,
        [
            shape((16, 4, 32, 256)), shape((16, 2, 16, 256)), shape((16, 8, 256)), shape((8, 4, 256)),
            shape((2, 8, 16, 640)), shape((2, 16, 16, 640)),
        ],
        [
            buffer(1280, 3584), buffer(4, 80, 2, 2, 640), buffer(4, 80, 2, 2, 640),
            buffer(8, 16, 1280), buffer(8, 16, 1280), buffer(8, 16, 1280),
            buffer(8, 16, 1280), buffer(2, 16, 1280),
            buffer(SMALL, 256), buffer(SMALL, 256), buffer(SMALL, 256), buffer(SMALL, 256),
            buffer(COT, 256), buffer(COT, 256), buffer(8, 8, 16, 256), buffer(8, 8, 16, 256),
            buffer(TOK, 1280), buffer(4, 256, 640), buffer(4, 4, RING, 256), buffer(2, 2, RING, 256),
            wide(OWN, 1280), buffer(4, TOK, 640), wide(4, OWN, 640), wide(4, OWN, 640), wide(4, OWN, 1),
            buffer(6, 6, TOK, 256), buffer(6, 6, TOK, 256), wide(4, 4, OWN, 256), wide(4, 4, OWN, 1),
            buffer(5, 4, OWN, 256), buffer(OWN, 3584), buffer(4, 4, OWN, 256), buffer(2, 2, OWN, 256),
            buffer(256, 1024),
            buffer(2, 8, 16, 640), buffer(2, 8, 16, 640), buffer(2, 8, 8, 16, 640),
            buffer(2, 16, 16, 640), buffer(2, 16, 16, 640),
            pltpu.SemaphoreType.DMA((copies,)), pltpu.SemaphoreType.DMA((copies,)),
            pltpu.SemaphoreType.DMA((2, 4)),
        ],
        args,
        collective_id=0,
        specs=specs,
    )


def finish_kernel(home, parts, *levels_and_outs):
    ins, (grads, weight), outs = levels_and_outs[:4], levels_and_outs[4:6], levels_and_outs[6:]
    for h in range(2):
        cols = slice(640 * h, 640 * h + 640)
        for j in range(8):
            for i in range(2):
                grads[64 * i + 8 * j : 64 * i + 8 * j + 8, cols] = home[h, j, 8 * i : 8 * i + 8]
        total = parts[h, 0].astype(F32)
        for j in range(1, 16):
            total = total + parts[h, j].astype(F32)
        weight[:, cols] = total[:10]
    for level_in, level_out in zip(ins, outs):
        level_out[...] = level_in[...]


def finish(home, parts, *levels):
    return call(
        finish_kernel,
        [shape((OWN, 1280)), shape((10, 1280), F32)] + [shape(level.shape) for level in levels],
        [],
        (home, parts) + levels,
    )


def body(
    features,
    attn_hidden,
    first_deconv,
    first_bias,
    mid_gain,
    mid_shift,
    second_deconv,
    second_bias,
    half_deconv,
    half_bias,
    lateral_four,
    lateral_eight,
    lateral_sixteen,
    lateral_coarse,
    output_conv,
    level_gain,
    level_shift,
    cotangent_four,
    cotangent_eight,
    cotangent_sixteen,
    cotangent_coarse,
):
    k2t = second_deconv.transpose(1, 2, 3, 0).reshape(4, 320, 640)
    conv = output_conv.reshape(4, 9, 256, 256)
    cot4 = cotangent_four.reshape(16, 4, 32, 256)
    cot8 = cotangent_eight.reshape(16, 2, 16, 256)
    quads = quad_pick()
    rings = cot_ring(4), cot_ring(2)
    split4, split8 = (const(np.stack([interleave(n), interleave(n).T])) for n in (4, 2))
    out4, out8, lev16, levc, home, parts = main(
        features[0], attn_hidden[0], first_deconv, half_deconv, k2t,
        lateral_four, lateral_eight, lateral_sixteen, lateral_coarse, second_bias, half_bias,
        conv, level_gain, level_shift, cot4, cot8, cotangent_sixteen[0], cotangent_coarse[0],
        const(chunk_split()), const(column_pick()), const(ring_pick()), const(small_send()),
        const(small_taps()), const(quads), const(quads.transpose(0, 2, 1)), const(cot_pick()),
        const(rings[0]), const(rings[1]),
        const(shift_matrices().reshape(9, TOK, TOK)), split4, split8,
        first_bias, mid_gain, mid_shift,
    )
    grads, weight, out4, out8, lev16, levc = finish(home, parts, out4, out8, lev16, levc)
    return (
        out4.reshape(1, 64, 32, 256),
        out8.reshape(1, 32, 16, 256),
        lev16[None],
        levc[None],
        grads[None],
        weight,
    )


def solution(mesh):
    tokens = P("segment", ("tr", "tc"), None)
    deconv = P("segment", None, None, None)
    grid = P("segment", "tr", "tc", None)
    placed = (
        (tokens, tokens, deconv) + (P(),) * 5 + (deconv,) + (P(),) * 8 + (grid,) * 4
    )
    return jax.shard_map(
        body,
        mesh=mesh,
        in_specs=placed,
        out_specs=(grid, grid, grid, grid, tokens, P(("segment", "tr", "tc"), None)),
        check_vma=False,
    )
```
